128 devices in a mesh: reg: 64 (over x, y, z), col: 2 (over core).
Axes of the slice: x: 4, y: 4, z: 4, core: 2. Of those that a mesh axis runs over, the one named last changes fastest.
Arguments:
- innovation: float32 [64, 524288], P(None, ('reg', 'col')), may hold values from -6 to 6
- obs_along: float32 [524288], P(('reg', 'col')), may hold values from 0 to 2
- obs_across: float32 [524288], P(('reg', 'col')), may hold values from 0 to 32
- obs_scale: float32 [524288], P(('reg', 'col')), may hold values from 0.5 to 2
- obs_error: float32 [524288], P(('reg', 'col')), may hold values from 0.1 to 1
- obs_gain: float32 [524288], P(('reg', 'col')), may hold values from 0.3 to 3
- pair_live: int32 [512, 2], P(('reg', 'col')), may hold values 0 or 1
- obs_count: int32 [512], P(('reg', 'col')), may hold values from 256 to 1024, as said below
- col_owner: int32 [524288], P(('reg', 'col')), may hold values from 0 to 131071, as said below
Outputs:
- weights: float32 [64, 524288], P(None, ('reg', 'col'))
- increments: float32 [64, 131072], P(None, ('reg', 'col'))
The draws below stay inside these ranges and needn't reach their ends.
Inputs may be any that keep to these rules, and one draw needn't show every extreme that they name: `obs_count`: slots of a region block at or after its count are empty. Some region holds 1024 observations and some holds 256. `col_owner`: observation slot o lies in device block k = o // 4096, and its column is one of k * 1024 to k * 1024 + 2 * 1024 - 1, taken modulo 131072; column block k belongs to the same position k in the order of devices.
All inputs are finite; a program needn't handle non-finite values. No bound on the sum of `pair_live` on one device may be relied on, other than what follows from the above.
Results may differ from the reference program's by a relative error of at most 0.0003.
Values sent between devices are 32-bit elements; how exact they have to be, the bound alone decides.
No kernel may reach another device: no remote copies, remote signals or barrier semaphores. Data moves between devices by JAX's collectives and lax.ppermute only.
A program may use at most 64 MiB of HBM per device.

```python
import math
import jax
import jax.numpy as jnp
from jax import lax

ENS = 64
ROWS = 1024
REACH = 2
ITERS = 2
REG_DEV = 4
COLS_DEV = 1024
NREG = 512
NOBS = 524288
NCOL = 131072


def draw_obs_count(key, part):
    counts = jax.random.randint(jax.random.fold_in(key, 11), (NREG,), ROWS // 4, ROWS + 1)
    full_region = jax.random.randint(jax.random.fold_in(key, 12), (), 0, NREG)
    shift_draw = jax.random.randint(jax.random.fold_in(key, 13), (), 1, NREG)
    least_region = (full_region + shift_draw) % NREG
    region_ids = jnp.arange(NREG, dtype=jnp.int32)
    counts = jnp.where(region_ids == full_region, ROWS, counts)
    counts = jnp.where(region_ids == least_region, ROWS // 4, counts)
    return counts.astype(jnp.int32)


def draw_col_owner(key, part):
    owner_block = jnp.arange(NOBS, dtype=jnp.int32) // (REG_DEV * ROWS)
    offset_draw = jax.random.randint(jax.random.fold_in(key, 21), (NOBS,), 0, 2 * COLS_DEV)
    return ((owner_block * COLS_DEV + offset_draw) % NCOL).astype(jnp.int32)


def set_ends(values, rng, smallest, largest):
    place = [jax.random.randint(jax.random.fold_in(rng, axis), (), 0, length) for axis, length in enumerate(values.shape)]
    main_axis = values.shape.index(max(values.shape))
    neighbour = place[:main_axis] + [(place[main_axis] + 1) % values.shape[main_axis]] + place[main_axis + 1:]
    return values.at[tuple(place)].set(smallest).at[tuple(neighbour)].set(largest)


def shard_levels(rng, shape, shards, least, top_value):
    factor_of = 1.0
    for dim, blocks in shards:
        heights = jax.random.uniform(jax.random.fold_in(jax.random.fold_in(rng, 6), dim), (blocks,), jnp.float32, least / len(shards), top_value / len(shards))
        factor_of = factor_of * jnp.repeat(jnp.exp(heights), shape[dim] // blocks).reshape((-1,) + (1,) * (len(shape) - 1 - dim))
    return factor_of


def gaussian(rng, dims, scale, bound, shards=(), held_as=jnp.bfloat16):
    result = scale * jax.random.normal(rng, dims, jnp.float32)
    if shards:
        result = result * shard_levels(rng, dims, shards, -0.22, 0.18)
    return jnp.clip(result, -bound, bound).astype(held_as)


def setup_inputs(seed: int = 0) -> dict:
    streams_of = jax.random.split(jax.random.key(seed), 10)
    return {
        "innovation": gaussian(streams_of[0], (ENS, NOBS), 1.0, 6.0, ((1, 128),), jnp.float32),
        "obs_along": jnp.clip(2.0 * jax.random.uniform(streams_of[1], (NOBS,), jnp.float32) ** shard_levels(streams_of[1], (NOBS,), ((0, 128),), -0.2, 0.2), 0.0, 2.0),
        "obs_across": jnp.clip(32.0 * jax.random.uniform(streams_of[2], (NOBS,), jnp.float32) ** shard_levels(streams_of[2], (NOBS,), ((0, 128),), -0.2, 0.2), 0.0, 32.0),
        "obs_scale": jnp.clip(jnp.exp(math.log(2.0) - 1.3862944 * jax.random.uniform(streams_of[3], (NOBS,), jnp.float32) ** shard_levels(streams_of[3], (NOBS,), ((0, 128),), -0.2, 0.2)), 0.5, 2.0),
        "obs_error": jnp.clip(jnp.exp(math.log(1.0) - 2.3025851 * jax.random.uniform(streams_of[4], (NOBS,), jnp.float32) ** shard_levels(streams_of[4], (NOBS,), ((0, 128),), -0.2, 0.2)), 0.1, 1.0),
        "obs_gain": jnp.clip(jnp.exp(math.log(3.0) - 2.3025851 * jax.random.uniform(streams_of[5], (NOBS,), jnp.float32) ** shard_levels(streams_of[5], (NOBS,), ((0, 128),), -0.2, 0.2)), 0.3, 3.0),
        "pair_live": set_ends((jax.random.randint(streams_of[6], (NREG, REACH), 0, 4) < 3).astype(jnp.int32), jax.random.fold_in(streams_of[6], 1), 0, 1),
        "obs_count": draw_obs_count(jax.random.fold_in(streams_of[9], 71), 0),
        "col_owner": draw_col_owner(jax.random.fold_in(streams_of[9], 71), 0),
    }


support_radius = 1.0
norm_scale = 16.0
highest = lax.Precision.HIGHEST

def support_shape(row_along, row_across, col_along, col_across, offset):
    delta_along = offset + col_along[None, :] - row_along[:, None]
    delta_across = col_across[None, :] - row_across[:, None]
    scaled_dist = jnp.minimum(jnp.sqrt(delta_along * delta_along + delta_across * delta_across) / support_radius, 1.0)
    return (1.0 - scaled_dist) ** 4 * (4.0 * scaled_dist + 1.0)

def cov_block(row_meta, col_meta, offset, factor):
    shape_part = support_shape(row_meta[0], row_meta[1], col_meta[0], col_meta[1], offset)
    return row_meta[2][:, None] * col_meta[2][None, :] * (shape_part * (factor / norm_scale))

def gram_matrix(lhs_rows, rhs_rows):
    return lax.dot_general(lhs_rows.astype(jnp.float32), rhs_rows.astype(jnp.float32), (((1,), (1,)), ((), ())), precision=highest, preferred_element_type=jnp.float32)

def combine_rows(coefficients, blocks):
    return lax.dot_general(coefficients.astype(jnp.float32), blocks.astype(jnp.float32), (((0,), (0,)), ((), ())), precision=highest, preferred_element_type=jnp.float32)

def symmetric(matrix):
    return 0.5 * (matrix + matrix.T)

def spd_solve(matrix, right_side):
    lower_factor = jnp.linalg.cholesky(matrix)
    return jax.scipy.linalg.cho_solve((lower_factor, True), right_side)

def operate(vectors, obs_along, obs_across, weight, factors, obs_error):
    blocks = vectors.reshape(ENS, NREG, ROWS)
    along_blocks = obs_along.reshape(NREG, ROWS)
    across_blocks = obs_across.reshape(NREG, ROWS)
    weight_blocks = weight.reshape(NREG, ROWS)
    summed = (obs_error[None, :] * vectors).reshape(ENS, NREG, ROWS)
    for offset in range(REACH + 1):

        def one_pair(region, offset=offset):
            partner = (region + offset) % NREG
            row_meta = (along_blocks[region], across_blocks[region], weight_blocks[region])
            col_meta = (along_blocks[partner], across_blocks[partner], weight_blocks[partner])
            factor = 1.0 if offset == 0 else factors[region, offset - 1]
            cov_tile = cov_block(row_meta, col_meta, offset, factor)
            to_self = gram_matrix(blocks[:, partner], cov_tile)
            if offset == 0:
                return (to_self, to_self)
            to_partner = jnp.dot(blocks[:, region].astype(jnp.float32), cov_tile.astype(jnp.float32), precision=highest, preferred_element_type=jnp.float32)
            return (to_self, to_partner)
        to_self, to_partner = lax.map(one_pair, jnp.arange(NREG, dtype=jnp.int32))
        summed = summed + jnp.transpose(to_self, (1, 0, 2))
        if offset > 0:
            summed = summed + jnp.transpose(jnp.roll(to_partner, offset, axis=0), (1, 0, 2))
    return summed.reshape(ENS, NOBS)

def reference(innovation, obs_along, obs_across, obs_scale, obs_error, obs_gain, pair_live, obs_count, col_owner):
    live_mask = (jnp.arange(ROWS, dtype=jnp.int32)[None, :] < obs_count[:, None]).astype(jnp.float32).reshape(NOBS)
    weight = obs_scale * live_mask
    factors = pair_live.astype(jnp.float32)
    residual = innovation * live_mask[None, :]
    solution = jnp.zeros_like(residual)
    direction = residual
    norm_now = symmetric(gram_matrix(residual, residual))
    for iteration in range(ITERS):
        images = operate(direction, obs_along, obs_across, weight, factors, obs_error)
        curvature = symmetric(gram_matrix(direction, images))
        step_size = spd_solve(curvature, norm_now)
        solution = solution + combine_rows(step_size, direction)
        residual = residual - combine_rows(step_size, images)
        if iteration + 1 < ITERS:
            norm_next = symmetric(gram_matrix(residual, residual))
            conjugate = spd_solve(norm_now, norm_next)
            direction = residual + combine_rows(conjugate, direction)
            norm_now = norm_next
    scaled = solution * obs_gain[None, :]
    increments = jax.ops.segment_sum(scaled.T, col_owner, num_segments=NCOL).T
    return (solution, increments)
```

```python
import jax
import jax.numpy as jnp
from jax import lax
from jax.sharding import PartitionSpec as P

ROWS = 1024
REACH = 2
COLS_DEV = 1024
AXES = ("reg", "col")
norm_scale = 16.0
highest = lax.Precision.HIGHEST


def from_behind(block, distance):
    size = lax.axis_size(AXES)
    return lax.ppermute(block, AXES, [((i - distance) % size, i) for i in range(size)])


def turned(block, stride, length, by):
    size = lax.axis_size(AXES)
    route = []
    for i in range(size):
        place = (i // stride) % length
        route.append((i, i + ((place + by) % length - place) * stride))
    return lax.ppermute(block, AXES, route)


def all_sum(block):
    size = lax.axis_size(AXES)
    stride = 1
    while stride < size:
        length = 2 if stride == 1 else min(4, size // stride)
        if length == 2:
            block = block + turned(block, stride, 2, 1)
        else:
            one = turned(block, stride, 4, 1)
            two = turned(block, stride, 4, 2)
            three = turned(block, stride, 4, 3)
            block = (block + two) + (one + three)
        stride *= length
    return block


def support_shape(row_along, row_across, col_along, col_across, offset):
    delta_along = offset + col_along[None, :] - row_along[:, None]
    delta_across = col_across[None, :] - row_across[:, None]
    scaled_dist = jnp.minimum(
        jnp.sqrt(delta_along * delta_along + delta_across * delta_across), 1.0
    )
    return (1.0 - scaled_dist) ** 4 * (4.0 * scaled_dist + 1.0)


def cov_block(row_meta, col_meta, offset, factor):
    shape_part = support_shape(row_meta[0], row_meta[1], col_meta[0], col_meta[1], offset)
    return row_meta[2][:, None] * col_meta[2][None, :] * (shape_part * (factor / norm_scale))


def dot(a, b, ca=1, cb=0):
    return lax.dot_general(
        a, b, (((ca,), (cb,)), ((), ())), precision=highest, preferred_element_type=jnp.float32
    )


def symmetric(matrix):
    return 0.5 * (matrix + matrix.T)


def spd_solve(matrix, right_side):
    lower_factor = jnp.linalg.cholesky(matrix)
    return jax.scipy.linalg.cho_solve((lower_factor, True), right_side)


def on_device(innovation, obs_along, obs_across, obs_scale, obs_error, obs_gain, pair_live, obs_count, col_owner):
    regions = obs_count.shape[0]
    local_rows = innovation.shape[1]
    reach_rows = REACH * ROWS
    live_mask = (
        (jnp.arange(ROWS, dtype=jnp.int32)[None, :] < obs_count[:, None])
        .astype(jnp.float32)
        .reshape(local_rows)
    )
    weight = obs_scale * live_mask
    factor_rows = jnp.repeat(pair_live.astype(jnp.float32).T, ROWS, axis=1)
    obs_meta = jnp.concatenate([jnp.stack([obs_along, obs_across, weight]), factor_rows], axis=0)
    meta_wide = jnp.concatenate([obs_meta, from_behind(obs_meta[:, :reach_rows], -1)], axis=1)
    resid = innovation * live_mask[None, :]

    def piece(a, start):
        return lax.dynamic_slice_in_dim(a, start, ROWS, 1)

    def tile(row_start, offset):
        rm = piece(meta_wide, row_start)
        cm = piece(meta_wide, row_start + offset * ROWS)
        f = 1.0 if offset == 0 else rm[2 + offset, 0]
        return cov_block(rm, cm, offset, f)

    def extend(v):
        return jnp.concatenate([v, from_behind(v[:, :reach_rows], -1)], axis=1)

    wide = extend(resid)

    def region_pass(region, totals):
        row_start = region * ROWS
        for offset in range(REACH + 1):
            partner = row_start + offset * ROWS
            c = tile(row_start, offset)
            cur = piece(totals, row_start)
            totals = lax.dynamic_update_slice_in_dim(
                totals, cur + dot(piece(wide, partner), c, 1, 1), row_start, 1
            )
            if offset > 0:
                cur = piece(totals, partner)
                totals = lax.dynamic_update_slice_in_dim(
                    totals, cur + dot(piece(wide, row_start), c, 1, 0), partner, 1
                )
        return totals

    totals = lax.fori_loop(
        0, regions, region_pass, jnp.zeros((resid.shape[0], local_rows + reach_rows), jnp.float32)
    )
    returned = from_behind(totals[:, local_rows:], 1)
    image = (
        jnp.concatenate([totals[:, :reach_rows] + returned, totals[:, reach_rows:local_rows]], axis=1)
        + obs_error[None, :] * resid
    )
    wide2 = extend(image)

    def second_pass(region, half):
        row_start = region * ROWS
        acc = 0.0
        for offset in range(REACH + 1):
            c = tile(row_start, offset) * (0.5 if offset == 0 else 1.0)
            acc = acc + dot(piece(wide2, row_start + offset * ROWS), c, 1, 1)
        return half + dot(piece(image, row_start), acc, 1, 1)

    half = lax.fori_loop(0, regions, second_pass, 0.5 * dot(image, obs_error[None, :] * image, 1, 1))

    gram = jnp.concatenate([dot(resid, resid, 1, 1), dot(resid, image, 1, 1), dot(image, image, 1, 1), half], axis=1)

    owner_base = lax.axis_index(AXES) * COLS_DEV
    total_cols = COLS_DEV * lax.axis_size(AXES)
    local_col = (col_owner - owner_base) % total_cols
    both = jnp.concatenate([resid, image], axis=0)
    scaled = both * obs_gain[None, :]
    slot_ids = jnp.arange(2 * COLS_DEV, dtype=jnp.int32)

    def column_pass(region, part):
        first = region * ROWS
        cols = lax.dynamic_slice_in_dim(local_col, first, ROWS, 0)
        one_hot = (cols[:, None] == slot_ids[None, :]).astype(jnp.float32)
        return part + dot(piece(scaled, first), one_hot)

    part = lax.fori_loop(0, regions, column_pass, jnp.zeros((both.shape[0], 2 * COLS_DEV), jnp.float32))
    col_sums = part[:, :COLS_DEV] + from_behind(part[:, COLS_DEV:], 1)

    gram = all_sum(gram)
    e = resid.shape[0]
    n0 = symmetric(gram[:, :e])
    k0 = symmetric(gram[:, e : 2 * e])
    m0 = symmetric(gram[:, 2 * e : 3 * e])
    l0 = gram[:, 3 * e :] + gram[:, 3 * e :].T
    s0 = spd_solve(k0, n0)
    ks = dot(k0, s0)
    n1 = symmetric(n0 - ks - ks.T + dot(s0, dot(m0, s0), 0, 0))
    b = jnp.eye(e, dtype=jnp.float32) + spd_solve(n0, n1)
    cross = dot(b, dot(m0, s0), 0, 0)
    c1 = symmetric(dot(b, dot(k0, b), 0, 0) - cross - cross.T + dot(s0, dot(l0, s0), 0, 0))
    s1 = spd_solve(c1, n1)
    mix = jnp.concatenate([s0 + dot(b, s1), -dot(s0, s1)], axis=0)
    return (dot(mix, both, 0, 0), dot(mix, col_sums, 0, 0))


def solution(mesh):
    row = P(None, AXES)
    vec = P(AXES)
    in_specs = (row, vec, vec, vec, vec, vec, P(AXES, None), vec, vec)
    return jax.shard_map(
        on_device, mesh=mesh, in_specs=in_specs, out_specs=(row, row), check_vma=False
    )
```

```python
import functools

import jax
import jax.numpy as jnp
from jax import lax
from jax.experimental import pallas as pl
from jax.experimental.pallas import tpu as pltpu
from jax.sharding import PartitionSpec as P

ROWS = 1024
REACH = 2
ENS = 64
BLK = 128
NB = ROWS // BLK
COLS_DEV = 1024
AXES = ("reg", "col")
FAR = 40.0
TOP = 32.0
MARGIN = 1.0001
UNROLL = 4
f32 = jnp.float32
bf16 = jnp.bfloat16
highest = lax.Precision.HIGHEST


def from_behind(block, distance):
    size = lax.axis_size(AXES)
    return lax.ppermute(block, AXES, [((i - distance) % size, i) for i in range(size)])


def turned(block, stride, length, by):
    size = lax.axis_size(AXES)
    route = []
    for i in range(size):
        place = (i // stride) % length
        route.append((i, i + ((place + by) % length - place) * stride))
    return lax.ppermute(block, AXES, route)


def all_sum(block):
    size = lax.axis_size(AXES)
    stride = 1
    while stride < size:
        length = 2 if stride == 1 else min(4, size // stride)
        if length == 2:
            block = block + turned(block, stride, 2, 1)
        else:
            one = turned(block, stride, 4, 1)
            two = turned(block, stride, 4, 2)
            three = turned(block, stride, 4, 3)
            block = (block + two) + (one + three)
        stride *= length
    return block


def dot(a, b, ca=1, cb=0, precision=None):
    return lax.dot_general(
        a, b, (((ca,), (cb,)), ((), ())), precision=precision, preferred_element_type=f32
    )


def iota(shape, dim):
    return lax.broadcasted_iota(jnp.int32, shape, dim)


def split(x):
    hi = x.astype(bf16)
    return hi, (x - hi.astype(f32)).astype(bf16)


def params(mib, **kw):
    return pltpu.CompilerParams(vmem_limit_bytes=mib << 20, **kw)


def cost(flops, moved):
    return pl.CostEstimate(flops=flops, bytes_accessed=moved, transcendentals=0)


SMEM = pl.BlockSpec(memory_space=pltpu.SMEM)
VMEM = pl.BlockSpec(memory_space=pltpu.VMEM)


def sort_kernel(count, pair, meta, innov, row_out, col_out, res_out, wres_out):
    g = pl.program_id(0)
    idx = iota((1, ROWS), 1)
    live = idx < count[g]
    along, scale, err = meta[0:1, :], meta[2:3, :], meta[3:4, :]
    key = jnp.where(live, meta[1:2, :], FAR)
    key_col = jnp.transpose(jnp.broadcast_to(key, (8, ROWS)))
    rank = jnp.zeros((1, ROWS), f32)
    for b in range(NB):
        kc = key_col[b * BLK : (b + 1) * BLK, 0:1]
        ji = iota((BLK, 1), 0) + b * BLK
        before = (kc < key) | ((kc == key) & (ji < idx))
        rank = rank + jnp.sum(jnp.where(before, 1.0, 0.0), axis=0, keepdims=True)
    rank = rank.astype(jnp.int32)
    x = jnp.where(live, innov[...], 0.0)
    quarter = jnp.where(live, scale * 0.25, 0.0)
    m = jnp.concatenate([along, key, quarter, err], axis=0)
    xh, xr = x.astype(bf16), x - x.astype(bf16).astype(f32)
    xm, xl = split(xr)
    mh, mr = m.astype(bf16).astype(f32), m - m.astype(bf16).astype(f32)
    mm = mr.astype(bf16).astype(f32)
    ml = mr - mm
    metas = jnp.concatenate([mh, mm, ml, jnp.zeros((52, ROWS), f32)], axis=0).astype(bf16)
    data = jnp.concatenate([xh, xm, xl, metas], axis=0)
    step = 256
    for b in range(ROWS // step):
        pick = jnp.where(rank == iota((step, 1), 0) + b * step, 1.0, 0.0).astype(bf16)
        y = dot(pick, data, 1, 1)
        t0, t1 = y[:, :128], y[:, 128:]
        r = t0 + pltpu.roll(t0, 64, 1) + t1
        c = t1 + pltpu.roll(t1, 124, 1) + pltpu.roll(t1, 120, 1)
        rows = pl.ds(b * step, step)
        col_out[rows, :] = c
        u = r * c[:, 66:67]
        for s in range(2):

            @pl.when(g % 2 == s)
            def _(s=s, r=r, u=u, rows=rows):
                res_out[0, rows, s * ENS : (s + 1) * ENS] = r[:, :ENS]
                wres_out[0, rows, s * ENS : (s + 1) * ENS] = u[:, :ENS]

        row_out[0:4, rows] = jnp.transpose(c)[64:68, :]
    row_out[4:5, :] = rank.astype(f32)
    row_out[5:6, :] = jnp.full((1, ROWS), pair[2 * g], f32)
    row_out[6:7, :] = jnp.full((1, ROWS), pair[2 * g + 1], f32)
    row_out[7:8, :] = jnp.zeros((1, ROWS), f32)


def load_split(dst, first, packed):
    lane = iota((1, 128), 1) < ENS
    hi = packed.astype(bf16).astype(f32)
    lo = packed - hi
    dst[pl.ds(first, ROWS), :] = jnp.where(lane, hi, pltpu.roll(lo, 64, 1)).astype(bf16)
    dst[pl.ds(first + ROWS, ROWS), :] = jnp.where(lane, pltpu.roll(hi, 64, 1), lo).astype(bf16)


def list_pairs(todo, n, row_bounds, row_first, col_bounds, col_first, offset, go):
    def row_step(i, n):
        lo = row_bounds[0, row_first + i] - MARGIN
        hi = jnp.minimum(row_bounds[1, row_first + i], TOP) + MARGIN
        for j in range(NB):
            jlo = col_bounds[0, col_first + j]
            jhi = jnp.minimum(col_bounds[1, col_first + j], TOP)
            todo[n] = (row_first + i) + 64 * (col_first + j) + 4096 * (offset + REACH)
            n = n + jnp.where((jlo <= hi) & (jhi >= lo), 1, 0)
        return n

    if go is None:
        return lax.fori_loop(0, NB, row_step, n)
    return lax.fori_loop(0, jnp.where(go > 0.5, NB, 0), row_step, n)


def run_pairs(todo, start, n, col_meta, row_meta, halves, acc):
    trash = 32
    for u in range(UNROLL):
        todo[n + u] = trash + 4096 * REACH

    def group(t, _):
        out = []
        for u in range(UNROLL):
            code = todo[start + t * UNROLL + u]
            i = code & 63
            j = (code >> 6) & 63
            shift = ((code >> 12) - REACH).astype(f32)
            im = jnp.minimum(i, trash - 1)
            ri = pl.ds(pl.multiple_of(im * BLK, BLK), BLK)
            cj = pl.ds(pl.multiple_of(j * BLK, BLK), BLK)
            da = (row_meta[0:1, cj] + shift) - col_meta[ri, 64:65]
            db = row_meta[1:2, cj] - col_meta[ri, 65:66]
            s = jnp.minimum(jnp.maximum(da * da + db * db, 1e-30), 1.0)
            q = s * lax.rsqrt(s)
            t1 = 1.0 - q
            t2 = t1 * t1
            phi = t2 * t2 * (4.0 * q + 1.0)
            hi, lo = split(phi)
            w = halves[cj, :]
            out.append(
                (i, dot(jnp.concatenate([hi, lo], axis=1), jnp.concatenate([w, w], axis=0)))
            )
        for i, val in out:
            ro = pl.ds(pl.multiple_of(i * BLK, BLK), BLK)
            acc[ro, :] += val
        return 0

    lax.fori_loop(0, (n - start + UNROLL - 1) // UNROLL, group, 0)


def fold(acc, first):
    a = acc[pl.ds(first, ROWS), :]
    b = acc[pl.ds(first + ROWS, ROWS), :]
    lane = iota((1, 128), 1) < ENS
    return jnp.where(lane, a + pltpu.roll(a, 64, 1), b + pltpu.roll(b, 64, 1))


def near_kernel(regions, bounds, col_meta, row_meta, wres, out, todo, halves, acc):
    for p in range(regions // 2):
        load_split(halves, 2 * p * ROWS, wres[p])
    acc[...] = jnp.zeros_like(acc)
    n = jnp.int32(0)
    for g in range(regions):
        for d in range(-REACH, REACH + 1):
            h = g + d
            if 0 <= h < regions:
                go = None if d == 0 else bounds[1 + abs(d), min(g, h) * NB]
                n = list_pairs(todo, n, bounds, g * NB, bounds, h * NB, d, go)
    run_pairs(todo, 0, n, col_meta, row_meta, halves, acc)
    out[...] = acc[: regions * ROWS, :]


def far_kernel(regions, bounds, pbounds, nbounds, col_meta, prow, nrow, pres, nres, res, part,
               img_out, wimg_out, todo, halves, rowm, acc):
    span = REACH * ROWS
    load_split(halves, 0, pres[0])
    load_split(halves, span, nres[0])
    rowm[:, :span] = prow[...]
    rowm[:, span:] = nrow[...]
    acc[: regions * ROWS, :] = part[...]
    acc[regions * ROWS :, :] = jnp.zeros((BLK, 128), f32)
    n = jnp.int32(0)
    for g in range(REACH):
        for d in range(g + 1, REACH + 1):
            h = REACH + g - d
            n = list_pairs(todo, n, bounds, g * NB, pbounds, h * NB, -d, pbounds[1 + d, h * NB])
    lead = REACH * NB
    for k in range(REACH):
        g = regions - REACH + k
        for d in range(REACH - k, REACH + 1):
            h = g + d - regions

            def shifted(i, n, g=g, d=d, h=h):
                lo = bounds[0, g * NB + i] - MARGIN
                hi = jnp.minimum(bounds[1, g * NB + i], TOP) + MARGIN
                for j in range(NB):
                    jlo = nbounds[0, h * NB + j]
                    jhi = jnp.minimum(nbounds[1, h * NB + j], TOP)
                    todo[n] = (g * NB + i) + 64 * (lead + h * NB + j) + 4096 * (d + REACH)
                    n = n + jnp.where((jlo <= hi) & (jhi >= lo), 1, 0)
                return n

            n = lax.fori_loop(0, jnp.where(bounds[1 + d, g * NB] > 0.5, NB, 0), shifted, n)
    run_pairs(todo, 0, n, col_meta, rowm, halves, acc)
    lane = iota((1, 128), 1) < ENS
    for p in range(regions // 2):
        a = col_meta[pl.ds(2 * p * ROWS, ROWS), :]
        b = col_meta[pl.ds((2 * p + 1) * ROWS, ROWS), :]
        w = jnp.where(lane, a[:, 66:67], b[:, 66:67])
        e = jnp.where(lane, a[:, 67:68], b[:, 67:68])
        image = fold(acc, 2 * p * ROWS) * w + e * res[p]
        img_out[p] = image
        wimg_out[p] = image * w


def near2_kernel(regions, bounds, col_meta, row_meta, wimg, res, img, out, gram_out, todo, halves, acc):
    for p in range(regions // 2):
        load_split(halves, 2 * p * ROWS, wimg[p])
    acc[...] = jnp.zeros_like(acc)
    n = jnp.int32(0)
    for g in range(regions):
        n = list_pairs(todo, n, bounds, g * NB, bounds, g * NB, 0, None)
    run_pairs(todo, 0, n, col_meta, row_meta, halves, acc)
    out[...] = acc[: regions * ROWS, :] * 0.5
    acc[...] = jnp.zeros_like(acc)
    n = jnp.int32(0)
    for g in range(regions):
        for d in range(1, REACH + 1):
            if g + d < regions:
                n = list_pairs(todo, n, bounds, g * NB, bounds, (g + d) * NB, d, bounds[1 + d, g * NB])
    run_pairs(todo, 0, n, col_meta, row_meta, halves, acc)
    out[...] += acc[: regions * ROWS, :]
    lane = iota((1, 128), 1) < ENS
    gram = jnp.zeros((128, 128), f32)
    for p in range(regions // 2):
        r, i = res[p], img[p]
        one = jnp.where(lane, r, pltpu.roll(i, 64, 1))
        two = jnp.where(lane, pltpu.roll(r, 64, 1), i)
        gram = gram + dot(one, one, 0, 0, highest) + dot(two, two, 0, 0, highest)
    gram_out[...] = gram


def far2_kernel(regions, bounds, nbounds, col_meta, nrow, nimg, wimg, img, part, gram, out, todo, halves, acc):
    load_split(halves, 0, nimg[0])
    acc[: regions * ROWS, :] = part[...]
    acc[regions * ROWS :, :] = jnp.zeros((BLK, 128), f32)
    n = jnp.int32(0)
    for k in range(REACH):
        g = regions - REACH + k
        for d in range(REACH - k, REACH + 1):
            n = list_pairs(todo, n, bounds, g * NB, nbounds, (g + d - regions) * NB, d, bounds[1 + d, g * NB])
    run_pairs(todo, 0, n, col_meta, nrow, halves, acc)
    lane = iota((1, 128), 1) < ENS
    half = jnp.zeros((128, 128), f32)
    for p in range(regions // 2):
        a = col_meta[pl.ds(2 * p * ROWS, ROWS), :]
        b = col_meta[pl.ds((2 * p + 1) * ROWS, ROWS), :]
        e = jnp.where(lane, a[:, 67:68], b[:, 67:68])
        i = img[p]
        half = half + dot(wimg[p], fold(acc, 2 * p * ROWS), 0, 0, highest)
        half = half + 0.5 * dot(i, e * i, 0, 0, highest)
    out[:, 0:64] = gram[0:64, 0:64]
    out[:, 64:128] = gram[0:64, 64:128]
    out[:, 128:192] = gram[64:128, 64:128]
    out[:, 192:256] = half[0:64, 0:64] + half[64:128, 64:128]


def column_kernel(count, row_meta, raw, innov, img, both_out, sums_out):
    g = pl.program_id(0)
    live = iota((1, ROWS), 1) < count[g]
    r = jnp.where(live, innov[...], 0.0)
    t = jnp.transpose(img[0])
    t = jnp.where(g % 2 == 0, t[:ENS, :], t[ENS:, :])
    hi, lo = split(t)
    lhs = jnp.concatenate([hi, lo], axis=0)
    rank = row_meta[4:5, :].astype(jnp.int32)
    step = 256
    total = jnp.zeros((2 * ENS, ROWS), f32)
    for b in range(ROWS // step):
        put = jnp.where(rank == iota((step, 1), 0) + b * step, 1.0, 0.0).astype(bf16)
        total = total + dot(lhs[:, b * step : (b + 1) * step], put)
    image = total[:ENS, :] + total[ENS:, :]
    both = jnp.concatenate([r, image], axis=0)
    both_out[...] = both
    hi, lo = split(both * raw[4:5, :])
    lhs = jnp.concatenate([hi, lo], axis=0)
    owner = raw[5:6, :].astype(jnp.int32)

    @pl.when(g == 0)
    def _():
        sums_out[...] = jnp.zeros_like(sums_out)

    for b in range(2 * COLS_DEV // step):
        own = jnp.where(owner == iota((step, 1), 0) + b * step, 1.0, 0.0).astype(bf16)
        y = dot(lhs, own, 1, 1)
        sums_out[:, b * step : (b + 1) * step] += y[: 2 * ENS, :] + y[2 * ENS :, :]


def eliminate(pairs):
    work = [jnp.concatenate([a, b], axis=1) for a, b in pairs]
    rows = iota((ENS, 1), 0)
    for k in range(ENS):
        for p in range(len(work)):
            a = work[p]
            pivot = a[k : k + 1, k : k + 1]
            inv = 1.0 / pivot
            inv = inv * (2.0 - pivot * inv)
            row = a[k : k + 1, :] * inv
            work[p] = jnp.where(rows == k, row, a - a[:, k : k + 1] * row)
    return [a[:, ENS:] for a in work]


def finish_kernel(gram, both, sums, carried, weights_out, incr_out):
    g = gram[...]
    hd = functools.partial(dot, precision=highest)

    def sym(a):
        return 0.5 * (a + jnp.transpose(a))

    n0 = sym(g[:, 0:64])
    k0 = sym(g[:, 64:128])
    m0 = sym(g[:, 128:192])
    l0 = g[:, 192:256] + jnp.transpose(g[:, 192:256])
    eye = jnp.where(iota((ENS, ENS), 0) == iota((ENS, ENS), 1), 1.0, 0.0)
    s0, inv = eliminate([(k0, n0), (n0, eye)])
    s0t = jnp.transpose(s0)
    ks = hd(k0, s0)
    ms = hd(m0, s0)
    n1 = sym(n0 - ks - jnp.transpose(ks) + hd(s0t, ms))
    b = eye + hd(inv, n1)
    bt = jnp.transpose(b)
    cross = hd(bt, ms)
    c1 = sym(hd(bt, hd(k0, b)) - cross - jnp.transpose(cross) + hd(s0t, hd(l0, s0)))
    (s1,) = eliminate([(c1, n1)])
    mix = jnp.concatenate([s0 + hd(b, s1), -hd(s0, s1)], axis=0)
    mt = jnp.transpose(mix)
    hi, lo = split(mt)
    lhs = jnp.concatenate([hi, hi, lo], axis=1)

    def apply(x):
        xh, xl = split(x)
        return dot(lhs, jnp.concatenate([xh, xl, xh], axis=0))

    step = 512
    for c in range(weights_out.shape[1] // step):
        at = pl.ds(c * step, step)
        weights_out[:, at] = apply(both[:, at])
    for c in range(COLS_DEV // step):
        at = pl.ds(c * step, step)
        incr_out[:, at] = apply(sums[:, at] + carried[:, at])


def bounds_of(row_meta):
    s = row_meta.reshape(8, -1, BLK)
    return jnp.stack([s[1, :, 0], s[1, :, BLK - 1], s[5, :, 0], s[6, :, 0]])


def on_device(innovation, obs_along, obs_across, obs_scale, obs_error, obs_gain, pair_live, obs_count, col_owner):
    regions = obs_count.shape[0]
    local = regions * ROWS
    packs = regions // 2
    span = REACH * ROWS
    total_cols = COLS_DEV * lax.axis_size(AXES)
    owner = (col_owner - lax.axis_index(AXES) * COLS_DEV) % total_cols
    zero = jnp.zeros((local,), f32)
    raw = jnp.stack(
        [obs_along, obs_across, obs_scale, obs_error, obs_gain, owner.astype(f32), zero, zero]
    )
    pairs = pair_live.astype(f32).reshape(-1)
    shape = jax.ShapeDtypeStruct
    packed = shape((packs, ROWS, 128), f32)
    row_spec = pl.BlockSpec((8, ROWS), lambda g: (0, g))
    pack_spec = pl.BlockSpec((1, ROWS, 128), lambda g: (g // 2, 0, 0))
    member_spec = pl.BlockSpec((ENS, ROWS), lambda g: (0, g))
    row_meta, col_meta, res, wres = pl.pallas_call(
        sort_kernel,
        grid=(regions,),
        in_specs=[SMEM, SMEM, row_spec, member_spec],
        out_specs=[row_spec, pl.BlockSpec((ROWS, 128), lambda g: (g, 0)), pack_spec, pack_spec],
        out_shape=[shape((8, local), f32), shape((local, 128), f32), packed, packed],
        compiler_params=params(24),
        name="order",
    )(obs_count, pairs, raw, innovation)

    prow = from_behind(row_meta[:, local - span :], 1)
    nrow = from_behind(row_meta[:, :span], -1)
    pres = from_behind(wres[packs - 1 :], 1)
    nres = from_behind(wres[:1], -1)
    bounds = bounds_of(row_meta)
    pbounds = bounds_of(prow)
    nbounds = bounds_of(nrow)
    todo = pltpu.SMEM((20 * 64 + 8,), jnp.int32)
    acc = pltpu.VMEM((local + BLK, 128), f32)
    plain = shape((local, 128), f32)

    part = pl.pallas_call(
        functools.partial(near_kernel, regions),
        in_specs=[SMEM, VMEM, VMEM, VMEM],
        out_specs=VMEM,
        out_shape=plain,
        scratch_shapes=[todo, pltpu.VMEM((local, 128), bf16), acc],
        compiler_params=params(24),
        cost_estimate=cost(int(4e9), int(2e7)),
        name="near",
    )(bounds, col_meta, row_meta, wres)
    img, wimg = pl.pallas_call(
        functools.partial(far_kernel, regions),
        in_specs=[SMEM] * 3 + [VMEM] * 7,
        out_specs=[VMEM, VMEM],
        out_shape=[packed, packed],
        scratch_shapes=[todo, pltpu.VMEM((2 * span, 128), bf16), pltpu.VMEM((8, 2 * span), f32), acc],
        compiler_params=params(24),
        name="far",
    )(bounds, pbounds, nbounds, col_meta, prow, nrow, pres, nres, res, part)
    nimg = from_behind(wimg[:1], -1)
    part2, gram = pl.pallas_call(
        functools.partial(near2_kernel, regions),
        in_specs=[SMEM] + [VMEM] * 5,
        out_specs=[VMEM, VMEM],
        out_shape=[plain, shape((128, 128), f32)],
        scratch_shapes=[todo, pltpu.VMEM((local, 128), bf16), acc],
        compiler_params=params(24),
        cost_estimate=cost(int(4e9), int(2e7)),
        name="near_again",
    )(bounds, col_meta, row_meta, wimg, res, img)
    gram = pl.pallas_call(
        functools.partial(far2_kernel, regions),
        in_specs=[SMEM] * 2 + [VMEM] * 7,
        out_specs=VMEM,
        out_shape=shape((ENS, 4 * ENS), f32),
        scratch_shapes=[todo, pltpu.VMEM((span, 128), bf16), acc],
        compiler_params=params(24),
        name="far_again",
    )(bounds, nbounds, col_meta, nrow, nimg, wimg, img, part2, gram)

    both, sums = pl.pallas_call(
        column_kernel,
        grid=(regions,),
        in_specs=[SMEM, row_spec, row_spec, member_spec, pack_spec],
        out_specs=[pl.BlockSpec((2 * ENS, ROWS), lambda g: (0, g)), pl.BlockSpec((2 * ENS, 2 * COLS_DEV), lambda g: (0, 0))],
        out_shape=[shape((2 * ENS, local), f32), shape((2 * ENS, 2 * COLS_DEV), f32)],
        compiler_params=params(24),
        cost_estimate=cost(int(8e9), int(2e7)),
        name="columns",
    )(obs_count, row_meta, raw, innovation, img)
    carried = from_behind(sums[:, COLS_DEV:], 1)

    gram = all_sum(gram)
    return tuple(
        pl.pallas_call(
            finish_kernel,
            in_specs=[VMEM] * 4,
            out_specs=[VMEM, VMEM],
            out_shape=[shape((ENS, local), f32), shape((ENS, COLS_DEV), f32)],
            compiler_params=params(24),
            name="finish",
        )(gram, both, sums, carried)
    )


def solution(mesh):
    row = P(None, AXES)
    vec = P(AXES)
    in_specs = (row, vec, vec, vec, vec, vec, P(AXES, None), vec, vec)
    return jax.shard_map(
        on_device, mesh=mesh, in_specs=in_specs, out_specs=(row, row), check_vma=False
    )
```

```python
import functools

import jax
import jax.numpy as jnp
from jax import lax
from jax.experimental import pallas as pl
from jax.experimental.pallas import tpu as pltpu
from jax.sharding import PartitionSpec as P

ROWS = 1024
REACH = 2
ENS = 64
BLK = 128
NB = ROWS // BLK
COLS_DEV = 1024
AXES = ("reg", "col")
FAR = 40.0
TOP = 32.0
MARGIN = 1.0001
PAIR_AT = 2 * NB
LIVE_AT = PAIR_AT + REACH
UNROLL = 8
GROUP = 4
f32 = jnp.float32
bf16 = jnp.bfloat16
highest = lax.Precision.HIGHEST


def from_behind(block, distance):
    size = lax.axis_size(AXES)
    return lax.ppermute(block, AXES, [((i - distance) % size, i) for i in range(size)])


def turned(block, stride, length, by):
    size = lax.axis_size(AXES)
    route = []
    for i in range(size):
        place = (i // stride) % length
        route.append((i, i + ((place + by) % length - place) * stride))
    return lax.ppermute(block, AXES, route)


def all_sum(block):
    size = lax.axis_size(AXES)
    stride = 1
    while stride < size:
        length = 2 if stride == 1 else min(4, size // stride)
        if length == 2:
            block = block + turned(block, stride, 2, 1)
        else:
            one = turned(block, stride, 4, 1)
            two = turned(block, stride, 4, 2)
            three = turned(block, stride, 4, 3)
            block = (block + two) + (one + three)
        stride *= length
    return block


def dot(a, b, ca=1, cb=0, precision=None):
    return lax.dot_general(
        a, b, (((ca,), (cb,)), ((), ())), precision=precision, preferred_element_type=f32
    )


def iota(shape, dim):
    return lax.broadcasted_iota(jnp.int32, shape, dim)


def split(x):
    hi = x.astype(bf16)
    return hi, (x - hi.astype(f32)).astype(bf16)


def params(mib, **kw):
    return pltpu.CompilerParams(vmem_limit_bytes=mib << 20, **kw)


def cost(flops, moved):
    return pl.CostEstimate(flops=flops, bytes_accessed=moved, transcendentals=0)


SMEM = pl.BlockSpec(memory_space=pltpu.SMEM)
VMEM = pl.BlockSpec(memory_space=pltpu.VMEM)


def sort_kernel(count, pair, meta, innov, row_out, col_out, along_out, across_out, res_out, wres_out):
    g = pl.program_id(0)
    idx = iota((1, ROWS), 1)
    live = idx < count[g]
    along, scale, err = meta[0:1, :], meta[2:3, :], meta[3:4, :]
    key = jnp.where(live, meta[1:2, :], FAR)
    key_col = jnp.transpose(jnp.broadcast_to(key, (8, ROWS)))
    rank = jnp.zeros((1, ROWS), f32)
    for b in range(NB):
        kc = key_col[b * BLK : (b + 1) * BLK, 0:1]
        at, end = b * BLK, (b + 1) * BLK
        here = key[:, at:end]
        tie = (kc == here) & (iota((BLK, BLK), 0) < iota((BLK, BLK), 1))
        counted = [jnp.where((kc < here) | tie, 1.0, 0.0)]
        if at > 0:
            counted.insert(0, jnp.where(kc < key[:, :at], 1.0, 0.0))
        if end < ROWS:
            counted.append(jnp.where(kc <= key[:, end:], 1.0, 0.0))
        rank = rank + jnp.concatenate(
            [jnp.sum(x, axis=0, keepdims=True) for x in counted], axis=1
        )
    rank = rank.astype(jnp.int32)
    x = jnp.where(live, innov[...], 0.0)
    quarter = jnp.where(live, scale * 0.25, 0.0)
    m = jnp.concatenate([along, key, quarter, err], axis=0)
    xh, xr = x.astype(bf16), x - x.astype(bf16).astype(f32)
    xm, xl = split(xr)
    mh, mr = m.astype(bf16).astype(f32), m - m.astype(bf16).astype(f32)
    mm = mr.astype(bf16).astype(f32)
    ml = mr - mm
    metas = jnp.concatenate([mh, mm, ml, jnp.zeros((52, ROWS), f32)], axis=0).astype(bf16)
    data = jnp.concatenate([xh, xm, xl, metas], axis=0)
    pick = jnp.where(rank == iota((ROWS, 1), 0), 1.0, 0.0).astype(bf16)
    ordered = dot(pick, data, 1, 1)
    step = 256
    for b in range(ROWS // step):
        y = ordered[b * step : (b + 1) * step, :]
        t0, t1 = y[:, :128], y[:, 128:]
        r = t0 + pltpu.roll(t0, 64, 1) + t1
        c = t1 + pltpu.roll(t1, 124, 1) + pltpu.roll(t1, 120, 1)
        rows = pl.ds(b * step, step)
        col_out[rows, :] = c
        along_out[rows, :] = jnp.broadcast_to(c[:, 64:65], (step, 128))
        across_out[rows, :] = jnp.broadcast_to(c[:, 65:66], (step, 128))
        u = r * c[:, 66:67]
        for s in range(2):

            @pl.when(g % 2 == s)
            def _(s=s, r=r, u=u, rows=rows):
                res_out[0, rows, s * ENS : (s + 1) * ENS] = r[:, :ENS]
                wres_out[0, rows, s * ENS : (s + 1) * ENS] = u[:, :ENS]

        row_out[0:4, rows] = jnp.transpose(c)[64:68, :]
    row_out[4:5, :] = rank.astype(f32)
    lane = iota((1, ROWS), 1)
    bound = jnp.where(lane == PAIR_AT, pair[g, 0], jnp.where(lane == PAIR_AT + 1, pair[g, 1], 0))
    bound = bound.astype(f32)
    bound = jnp.where(lane == LIVE_AT, ((count[g] + BLK - 1) // BLK).astype(f32), bound)
    for b in range(NB):
        first = row_out[1:2, b * BLK : b * BLK + 1]
        last = row_out[1:2, (b + 1) * BLK - 1 : (b + 1) * BLK]
        bound = jnp.where(lane == b, first, bound)
        bound = jnp.where(lane == NB + b, jnp.minimum(last, TOP), bound)
    row_out[5:8, :] = jnp.broadcast_to(bound, (3, ROWS))


def load_split(dst, first, packed):
    lane = iota((1, 128), 1) < ENS
    hi = packed.astype(bf16).astype(f32)
    lo = packed - hi
    dst[pl.ds(first, ROWS), :] = jnp.where(lane, hi, pltpu.roll(lo, 64, 1)).astype(bf16)
    dst[pl.ds(first + ROWS, ROWS), :] = jnp.where(lane, pltpu.roll(hi, 64, 1), lo).astype(bf16)


def list_pairs(todo, n, rows, row_at, cols, col_at, offset, go):
    jlo = [cols[7, j] for j in range(NB)]
    jhi = [cols[7, NB + j] for j in range(NB)]

    def row_step(i, n):
        lo = rows[7, i] - MARGIN
        hi = rows[7, NB + i] + MARGIN
        base = row_at + i + 4096 * (offset + REACH)
        for j in range(NB):
            todo[n] = base + 64 * (col_at + j)
            n = n + jnp.where((jlo[j] <= hi) & (jhi[j] >= lo), 1, 0)
        return n

    live = rows[7, LIVE_AT].astype(jnp.int32)
    if go is not None:
        live = jnp.where(go > 0.5, live, 0)
    return lax.fori_loop(0, live, row_step, n)


def run_pairs(todo, start, n, alongs, acrosses, row_meta, halves, acc):
    trash = 32
    for u in range(UNROLL):
        todo[n + u] = trash + 4096 * REACH

    def group(t, _):
        out = []
        for u in range(UNROLL):
            code = todo[start + t * UNROLL + u]
            i = code & 63
            j = (code >> 6) & 63
            shift = ((code >> 12) - REACH).astype(f32)
            im = jnp.minimum(i, trash - 1)
            ri = pl.ds(pl.multiple_of(im * BLK, BLK), BLK)
            cj = pl.ds(pl.multiple_of(j * BLK, BLK), BLK)
            da = (row_meta[0:1, cj] + shift) - alongs[ri, :]
            db = row_meta[1:2, cj] - acrosses[ri, :]
            s = jnp.minimum(jnp.maximum(da * da + db * db, 1e-30), 1.0)
            q = s * lax.rsqrt(s)
            t1 = 1.0 - q
            t2 = t1 * t1
            phi = t2 * t2 * (4.0 * q + 1.0)
            hi, lo = split(phi)
            w = halves[cj, :]
            out.append(
                (i, dot(jnp.concatenate([hi, lo], axis=1), jnp.concatenate([w, w], axis=0)))
            )
        for i, val in out:
            ro = pl.ds(pl.multiple_of(i * BLK, BLK), BLK)
            acc[ro, :] += val
        return 0

    lax.fori_loop(0, (n - start + UNROLL - 1) // UNROLL, group, 0)


def fold(acc, first):
    a = acc[pl.ds(first, ROWS), :]
    b = acc[pl.ds(first + ROWS, ROWS), :]
    lane = iota((1, 128), 1) < ENS
    return jnp.where(lane, a + pltpu.roll(a, 64, 1), b + pltpu.roll(b, 64, 1))


def flag(bounds, d):
    return bounds[7, PAIR_AT + d - 1]


def fetch_bounds(row_metas, scalars, sem):
    copies = []
    for ref in row_metas:
        for g in range(ref.shape[1] // ROWS):
            k = len(copies)
            src = ref.at[:, pl.ds(g * ROWS, BLK)]
            copies.append(pltpu.make_async_copy(src, scalars.at[k], sem.at[k]))
            copies[k].start()
    for c in copies:
        c.wait()
    return [scalars.at[k] for k in range(len(copies))]


def near_kernel(regions, alongs, acrosses, row_meta, wres, out, scalars, sem, todo, halves, acc):
    bounds = fetch_bounds([row_meta], scalars, sem)
    for p in range(regions // 2):
        load_split(halves, 2 * p * ROWS, wres[p])
    acc[...] = jnp.zeros_like(acc)
    n = jnp.int32(0)
    for g in range(regions):
        for d in range(-REACH, REACH + 1):
            h = g + d
            if 0 <= h < regions:
                go = None if d == 0 else flag(bounds[min(g, h)], abs(d))
                n = list_pairs(todo, n, bounds[g], g * NB, bounds[h], h * NB, d, go)
    run_pairs(todo, 0, n, alongs, acrosses, row_meta, halves, acc)
    out[...] = acc[: regions * ROWS, :]


def far_kernel(regions, col_meta, alongs, acrosses, row_meta, prow, nrow, pres, nres, res, part, img_out, wimg_out,
               scalars, sem, todo, halves, acc, rowm):
    bounds = fetch_bounds([row_meta, prow, nrow], scalars, sem)
    pbounds, nbounds = bounds[regions : regions + REACH], bounds[regions + REACH :]
    span = REACH * ROWS
    load_split(halves, 0, pres[0])
    load_split(halves, span, nres[0])
    rowm[:, :span] = prow[...]
    rowm[:, span:] = nrow[...]
    acc[: regions * ROWS, :] = part[...]
    acc[regions * ROWS :, :] = jnp.zeros((BLK, 128), f32)
    n = jnp.int32(0)
    for g in range(REACH):
        for d in range(g + 1, REACH + 1):
            h = REACH + g - d
            n = list_pairs(todo, n, bounds[g], g * NB, pbounds[h], h * NB, -d, flag(pbounds[h], d))
    for k in range(REACH):
        g = regions - REACH + k
        for d in range(REACH - k, REACH + 1):
            h = g + d - regions
            n = list_pairs(todo, n, bounds[g], g * NB, nbounds[h], (REACH + h) * NB, d, flag(bounds[g], d))
    run_pairs(todo, 0, n, alongs, acrosses, rowm, halves, acc)
    lane = iota((1, 128), 1) < ENS
    for p in range(regions // 2):
        a = col_meta[pl.ds(2 * p * ROWS, ROWS), :]
        b = col_meta[pl.ds((2 * p + 1) * ROWS, ROWS), :]
        w = jnp.where(lane, a[:, 66:67], b[:, 66:67])
        e = jnp.where(lane, a[:, 67:68], b[:, 67:68])
        image = fold(acc, 2 * p * ROWS) * w + e * res[p]
        img_out[p] = image
        wimg_out[p] = image * w


def near2_kernel(regions, alongs, acrosses, row_meta, wimg, res, img, out, gram_out,
                 scalars, sem, todo, halves, acc):
    bounds = fetch_bounds([row_meta], scalars, sem)
    for p in range(regions // 2):
        load_split(halves, 2 * p * ROWS, wimg[p])
    acc[...] = jnp.zeros_like(acc)
    n = jnp.int32(0)
    for g in range(regions):
        n = list_pairs(todo, n, bounds[g], g * NB, bounds[g], g * NB, 0, None)
    run_pairs(todo, 0, n, alongs, acrosses, row_meta, halves, acc)
    acc[...] = acc[...] * 0.5
    n = jnp.int32(0)
    for g in range(regions):
        for d in range(1, REACH + 1):
            if g + d < regions:
                go = flag(bounds[g], d)
                n = list_pairs(todo, n, bounds[g], g * NB, bounds[g + d], (g + d) * NB, d, go)
    run_pairs(todo, 0, n, alongs, acrosses, row_meta, halves, acc)
    out[...] = acc[: regions * ROWS, :]
    lane = iota((1, 128), 1) < ENS
    gram = jnp.zeros((128, 128), f32)
    for p in range(regions // 2):
        r, i = res[p], img[p]
        one = jnp.where(lane, r, pltpu.roll(i, 64, 1))
        two = jnp.where(lane, pltpu.roll(r, 64, 1), i)
        gram = gram + dot(one, one, 0, 0, highest) + dot(two, two, 0, 0, highest)
    gram_out[...] = gram


def far2_kernel(regions, col_meta, alongs, acrosses, row_meta, nrow, nimg, wimg, img, part, gram, out,
                scalars, sem, todo, halves, acc):
    bounds = fetch_bounds([row_meta, nrow], scalars, sem)
    nbounds = bounds[regions:]
    load_split(halves, 0, nimg[0])
    acc[: regions * ROWS, :] = part[...]
    acc[regions * ROWS :, :] = jnp.zeros((BLK, 128), f32)
    n = jnp.int32(0)
    for k in range(REACH):
        g = regions - REACH + k
        for d in range(REACH - k, REACH + 1):
            h = g + d - regions
            n = list_pairs(todo, n, bounds[g], g * NB, nbounds[h], h * NB, d, flag(bounds[g], d))
    run_pairs(todo, 0, n, alongs, acrosses, nrow, halves, acc)
    lane = iota((1, 128), 1) < ENS
    half = jnp.zeros((128, 128), f32)
    for p in range(regions // 2):
        a = col_meta[pl.ds(2 * p * ROWS, ROWS), :]
        b = col_meta[pl.ds((2 * p + 1) * ROWS, ROWS), :]
        e = jnp.where(lane, a[:, 67:68], b[:, 67:68])
        i = img[p]
        half = half + dot(wimg[p], fold(acc, 2 * p * ROWS), 0, 0, highest)
        half = half + 0.5 * dot(i, e * i, 0, 0, highest)
    out[:, 0:64] = gram[0:64, 0:64]
    out[:, 64:128] = gram[0:64, 64:128]
    out[:, 128:192] = gram[64:128, 64:128]
    out[:, 192:256] = half[0:64, 0:64] + half[64:128, 64:128]


def column_kernel(count, row_meta, raw, innov, img, both_out, sums_out):
    g = pl.program_id(0)
    live = iota((1, ROWS), 1) < count[g]
    r = jnp.where(live, innov[...], 0.0)
    t = jnp.transpose(img[0])
    t = jnp.where(g % 2 == 0, t[:ENS, :], t[ENS:, :])
    hi, lo = split(t)
    lhs = jnp.concatenate([hi, lo], axis=0)
    rank = row_meta[4:5, :].astype(jnp.int32)
    step = 256
    total = jnp.zeros((2 * ENS, ROWS), f32)
    for b in range(ROWS // step):
        put = jnp.where(rank == iota((step, 1), 0) + b * step, 1.0, 0.0).astype(bf16)
        total = total + dot(lhs[:, b * step : (b + 1) * step], put)
    image = total[:ENS, :] + total[ENS:, :]
    both = jnp.concatenate([r, image], axis=0)
    both_out[...] = both
    hi, lo = split(both * raw[4:5, :])
    lhs = jnp.concatenate([hi, lo], axis=0)
    owner = raw[5:6, :].astype(jnp.int32)

    @pl.when(g == 0)
    def _():
        sums_out[...] = jnp.zeros_like(sums_out)

    for b in range(2 * COLS_DEV // step):
        own = jnp.where(owner == iota((step, 1), 0) + b * step, 1.0, 0.0).astype(bf16)
        y = dot(lhs, own, 1, 1)
        sums_out[:, b * step : (b + 1) * step] += y[: 2 * ENS, :] + y[2 * ENS :, :]


def eliminate(pairs):
    work = [jnp.concatenate([a, b], axis=1) for a, b in pairs]
    index = iota((ENS, 2 * ENS), 0)
    for k in range(0, ENS, GROUP):
        for p in range(len(work)):
            a = work[p]
            cols = [jnp.broadcast_to(a[:, k + c : k + c + 1], a.shape) for c in range(GROUP)]
            rows = [a[k + i : k + i + 1, :] for i in range(GROUP)]
            e = [[cols[c][k + i : k + i + 1, :] for c in range(GROUP)] for i in range(GROUP)]
            inv = []
            for c in range(GROUP):
                guess = 1.0 / e[c][c]
                inv.append(guess * (2.0 - e[c][c] * guess))
                for i in range(c + 1, GROUP):
                    ratio = e[i][c] * inv[c]
                    for j in range(c + 1, GROUP):
                        e[i][j] = e[i][j] - ratio * e[c][j]
                    rows[i] = rows[i] - ratio * rows[c]
            for c in reversed(range(GROUP)):
                for j in range(c + 1, GROUP):
                    rows[c] = rows[c] - e[c][j] * rows[j]
                rows[c] = rows[c] * inv[c]
            for c in range(GROUP):
                a = a - cols[c] * rows[c]
            for c in range(GROUP):
                a = jnp.where(index == k + c, rows[c], a)
            work[p] = a
    return [a[:, ENS:] for a in work]


def finish_kernel(gram, both, sums, carried, weights_out, incr_out):
    g = gram[...]
    hd = functools.partial(dot, precision=highest)

    def sym(a):
        return 0.5 * (a + jnp.transpose(a))

    n0 = sym(g[:, 0:64])
    k0 = sym(g[:, 64:128])
    m0 = sym(g[:, 128:192])
    l0 = g[:, 192:256] + jnp.transpose(g[:, 192:256])
    eye = jnp.where(iota((ENS, ENS), 0) == iota((ENS, ENS), 1), 1.0, 0.0)
    s0, inv = eliminate([(k0, n0), (n0, eye)])
    s0t = jnp.transpose(s0)
    ks = hd(k0, s0)
    ms = hd(m0, s0)
    n1 = sym(n0 - ks - jnp.transpose(ks) + hd(s0t, ms))
    b = eye + hd(inv, n1)
    bt = jnp.transpose(b)
    cross = hd(bt, ms)
    c1 = sym(hd(bt, hd(k0, b)) - cross - jnp.transpose(cross) + hd(s0t, hd(l0, s0)))
    (s1,) = eliminate([(c1, n1)])
    mix = jnp.concatenate([s0 + hd(b, s1), -hd(s0, s1)], axis=0)
    mt = jnp.transpose(mix)
    hi, lo = split(mt)
    lhs = jnp.concatenate([hi, hi, lo], axis=1)

    def apply(x):
        xh, xl = split(x)
        return dot(lhs, jnp.concatenate([xh, xl, xh], axis=0))

    step = 512
    for c in range(weights_out.shape[1] // step):
        at = pl.ds(c * step, step)
        weights_out[:, at] = apply(both[:, at])
    for c in range(COLS_DEV // step):
        at = pl.ds(c * step, step)
        incr_out[:, at] = apply(sums[:, at] + carried[:, at])


def on_device(innovation, obs_along, obs_across, obs_scale, obs_error, obs_gain, pair_live, obs_count, col_owner):
    regions = obs_count.shape[0]
    local = regions * ROWS
    packs = regions // 2
    span = REACH * ROWS
    total_cols = COLS_DEV * lax.axis_size(AXES)
    owner = (col_owner - lax.axis_index(AXES) * COLS_DEV) % total_cols
    zero = jnp.zeros((local,), f32)
    raw = jnp.stack(
        [obs_along, obs_across, obs_scale, obs_error, obs_gain, owner.astype(f32), zero, zero]
    )
    shape = jax.ShapeDtypeStruct
    packed = shape((packs, ROWS, 128), f32)
    row_spec = pl.BlockSpec((8, ROWS), lambda g: (0, g))
    pack_spec = pl.BlockSpec((1, ROWS, 128), lambda g: (g // 2, 0, 0))
    member_spec = pl.BlockSpec((ENS, ROWS), lambda g: (0, g))
    row_meta, col_meta, alongs, acrosses, res, wres = pl.pallas_call(
        sort_kernel,
        grid=(regions,),
        in_specs=[SMEM, SMEM, row_spec, member_spec],
        out_specs=[row_spec] + [pl.BlockSpec((ROWS, 128), lambda g: (g, 0))] * 3 + [pack_spec] * 2,
        out_shape=[shape((8, local), f32)] + [shape((local, 128), f32)] * 3 + [packed] * 2,
        compiler_params=params(24),
        name="order",
    )(obs_count, pair_live, raw, innovation)

    prow = from_behind(row_meta[:, local - span :], 1)
    nrow = from_behind(row_meta[:, :span], -1)
    pres = from_behind(wres[packs - 1 :], 1)
    nres = from_behind(wres[:1], -1)
    def scratch(blocks):
        halos = regions + 2 * REACH
        return [
            pltpu.SMEM((halos, 8, BLK), f32),
            pltpu.SemaphoreType.DMA((halos,)),
            pltpu.SMEM((20 * 64 + 8,), jnp.int32),
            pltpu.VMEM((blocks * ROWS, 128), bf16),
            pltpu.VMEM((local + BLK, 128), f32),
        ]

    plain = shape((local, 128), f32)

    part = pl.pallas_call(
        functools.partial(near_kernel, regions),
        in_specs=[VMEM] * 4,
        out_specs=VMEM,
        out_shape=plain,
        scratch_shapes=scratch(regions),
        compiler_params=params(24),
        cost_estimate=cost(int(4e9), int(2e7)),
        name="near",
    )(alongs, acrosses, row_meta, wres)
    img, wimg = pl.pallas_call(
        functools.partial(far_kernel, regions),
        in_specs=[VMEM] * 10,
        out_specs=[VMEM, VMEM],
        out_shape=[packed, packed],
        scratch_shapes=scratch(2 * REACH) + [pltpu.VMEM((8, 2 * span), f32)],
        compiler_params=params(24),
        name="far",
    )(col_meta, alongs, acrosses, row_meta, prow, nrow, pres, nres, res, part)
    nimg = from_behind(wimg[:1], -1)
    part2, gram = pl.pallas_call(
        functools.partial(near2_kernel, regions),
        in_specs=[VMEM] * 6,
        out_specs=[VMEM, VMEM],
        out_shape=[plain, shape((128, 128), f32)],
        scratch_shapes=scratch(regions),
        compiler_params=params(24),
        cost_estimate=cost(int(4e9), int(2e7)),
        name="near_again",
    )(alongs, acrosses, row_meta, wimg, res, img)
    gram = pl.pallas_call(
        functools.partial(far2_kernel, regions),
        in_specs=[VMEM] * 10,
        out_specs=VMEM,
        out_shape=shape((ENS, 4 * ENS), f32),
        scratch_shapes=scratch(REACH),
        compiler_params=params(24),
        name="far_again",
    )(col_meta, alongs, acrosses, row_meta, nrow, nimg, wimg, img, part2, gram)

    both, sums = pl.pallas_call(
        column_kernel,
        grid=(regions,),
        in_specs=[SMEM, row_spec, row_spec, member_spec, pack_spec],
        out_specs=[pl.BlockSpec((2 * ENS, ROWS), lambda g: (0, g)), pl.BlockSpec((2 * ENS, 2 * COLS_DEV), lambda g: (0, 0))],
        out_shape=[shape((2 * ENS, local), f32), shape((2 * ENS, 2 * COLS_DEV), f32)],
        compiler_params=params(24),
        cost_estimate=cost(int(8e9), int(2e7)),
        name="columns",
    )(obs_count, row_meta, raw, innovation, img)
    carried = from_behind(sums[:, COLS_DEV:], 1)

    gram = all_sum(gram)
    return tuple(
        pl.pallas_call(
            finish_kernel,
            in_specs=[VMEM] * 4,
            out_specs=[VMEM, VMEM],
            out_shape=[shape((ENS, local), f32), shape((ENS, COLS_DEV), f32)],
            compiler_params=params(24),
            name="finish",
        )(gram, both, sums, carried)
    )


def solution(mesh):
    row = P(None, AXES)
    vec = P(AXES)
    in_specs = (row, vec, vec, vec, vec, vec, P(AXES, None), vec, vec)
    return jax.shard_map(
        on_device, mesh=mesh, in_specs=in_specs, out_specs=(row, row), check_vma=False
    )
```

```python
import functools

import jax
import jax.numpy as jnp
from jax import lax
from jax.experimental import pallas as pl
from jax.experimental.pallas import tpu as pltpu
from jax.sharding import PartitionSpec as P

ROWS = 1024
REACH = 2
ENS = 64
BLK = 128
NB = ROWS // BLK
COLS_DEV = 1024
AXES = ("reg", "col")
FAR = 40.0
TOP = 32.0
MARGIN = 1.0001
PAIR_AT = 2 * NB
LIVE_AT = PAIR_AT + REACH
UNROLL = 16
GROUP = 8
f32 = jnp.float32
bf16 = jnp.bfloat16
highest = lax.Precision.HIGHEST


def from_behind(block, distance):
    size = lax.axis_size(AXES)
    return lax.ppermute(block, AXES, [((i - distance) % size, i) for i in range(size)])


def turned(block, stride, length, by):
    size = lax.axis_size(AXES)
    route = []
    for i in range(size):
        place = (i // stride) % length
        route.append((i, i + ((place + by) % length - place) * stride))
    return lax.ppermute(block, AXES, route)


def all_sum(block, beside, make):
    size = lax.axis_size(AXES)
    stride = 1
    made = None
    while stride < size:
        length = 2 if stride == 1 else min(4, size // stride)
        if stride > 2 and made is None:
            block, beside = lax.optimization_barrier((block, beside))
            made = make(beside)
        if length == 2:
            block = block + turned(block, stride, 2, 1)
        else:
            one = turned(block, stride, 4, 1)
            two = turned(block, stride, 4, 2)
            three = turned(block, stride, 4, 3)
            block = (block + two) + (one + three)
        stride *= length
    return block, beside, make(beside) if made is None else made


def dot(a, b, ca=1, cb=0, precision=None):
    return lax.dot_general(
        a, b, (((ca,), (cb,)), ((), ())), precision=precision, preferred_element_type=f32
    )


def iota(shape, dim):
    return lax.broadcasted_iota(jnp.int32, shape, dim)


def split(x):
    hi = x.astype(bf16)
    return hi, (x - hi.astype(f32)).astype(bf16)


def params(mib, **kw):
    return pltpu.CompilerParams(vmem_limit_bytes=mib << 20, **kw)


def cost(flops, moved):
    return pl.CostEstimate(flops=flops, bytes_accessed=moved, transcendentals=0)


SMEM = pl.BlockSpec(memory_space=pltpu.SMEM)
VMEM = pl.BlockSpec(memory_space=pltpu.VMEM)


def sort_kernel(count, pair, meta, innov, row_out, col_out, along_out, across_out, res_out, wres_out):
    g = pl.program_id(0)
    idx = iota((1, ROWS), 1)
    live = idx < count[g]
    along, scale, err = meta[0:1, :], meta[2:3, :], meta[3:4, :]
    key = jnp.where(live, meta[1:2, :], FAR)
    key_col = jnp.transpose(jnp.broadcast_to(key, (8, ROWS)))
    rank = jnp.zeros((1, ROWS), f32)
    for b in range(NB):
        kc = key_col[b * BLK : (b + 1) * BLK, 0:1]
        at, end = b * BLK, (b + 1) * BLK
        here = key[:, at:end]
        tie = (kc == here) & (iota((BLK, BLK), 0) < iota((BLK, BLK), 1))
        counted = [jnp.where((kc < here) | tie, 1.0, 0.0)]
        if at > 0:
            counted.insert(0, jnp.where(kc < key[:, :at], 1.0, 0.0))
        if end < ROWS:
            counted.append(jnp.where(kc <= key[:, end:], 1.0, 0.0))
        rank = rank + jnp.concatenate(
            [jnp.sum(x, axis=0, keepdims=True) for x in counted], axis=1
        )
    rank = rank.astype(jnp.int32)
    x = jnp.where(live, innov[...], 0.0)
    quarter = jnp.where(live, scale * 0.25, 0.0)
    m = jnp.concatenate([along, key, quarter, err], axis=0)
    xh, xr = x.astype(bf16), x - x.astype(bf16).astype(f32)
    xm, xl = split(xr)
    mh, mr = m.astype(bf16).astype(f32), m - m.astype(bf16).astype(f32)
    mm = mr.astype(bf16).astype(f32)
    ml = mr - mm
    metas = jnp.concatenate([mh, mm, ml, jnp.zeros((52, ROWS), f32)], axis=0).astype(bf16)
    data = jnp.concatenate([xh, xm, xl, metas], axis=0)
    pick = jnp.where(rank == iota((ROWS, 1), 0), 1.0, 0.0).astype(bf16)
    ordered = dot(pick, data, 1, 1)
    step = 256
    for b in range(ROWS // step):
        y = ordered[b * step : (b + 1) * step, :]
        t0, t1 = y[:, :128], y[:, 128:]
        r = t0 + pltpu.roll(t0, 64, 1) + t1
        c = t1 + pltpu.roll(t1, 124, 1) + pltpu.roll(t1, 120, 1)
        rows = pl.ds(b * step, step)
        col_out[rows, :] = c
        along_out[rows, :] = jnp.broadcast_to(c[:, 64:65], (step, 128))
        across_out[rows, :] = jnp.broadcast_to(c[:, 65:66], (step, 128))
        u = r * c[:, 66:67]
        for s in range(2):

            @pl.when(g % 2 == s)
            def _(s=s, r=r, u=u, rows=rows):
                res_out[0, rows, s * ENS : (s + 1) * ENS] = r[:, :ENS]
                wres_out[0, rows, s * ENS : (s + 1) * ENS] = u[:, :ENS]

        row_out[0:4, rows] = jnp.transpose(c)[64:68, :]
    row_out[4:5, :] = rank.astype(f32)
    lane = iota((1, ROWS), 1)
    bound = jnp.where(lane == PAIR_AT, pair[g, 0], jnp.where(lane == PAIR_AT + 1, pair[g, 1], 0))
    bound = bound.astype(f32)
    bound = jnp.where(lane == LIVE_AT, ((count[g] + BLK - 1) // BLK).astype(f32), bound)
    for b in range(NB):
        first = row_out[1:2, b * BLK : b * BLK + 1]
        last = row_out[1:2, (b + 1) * BLK - 1 : (b + 1) * BLK]
        bound = jnp.where(lane == b, first, bound)
        bound = jnp.where(lane == NB + b, jnp.minimum(last, TOP), bound)
    row_out[5:8, :] = jnp.broadcast_to(bound, (3, ROWS))
    for s in range(2):

        @pl.when(g % 2 == s)
        def _(s=s):
            for b in range(NB):
                wres_out[0, meta_rows(s * NB + b), :] = row_out[:, b * BLK : (b + 1) * BLK]


def meta_rows(block):
    return pl.ds(ROWS + 8 * block, 8)


def unpack_meta(dst, first, packed):
    for b in range(2 * NB):
        dst[:, pl.ds((first + b) * BLK, BLK)] = packed[0, meta_rows(b), :]


def load_split(dst, first, packed):
    lane = iota((1, 128), 1) < ENS
    hi = packed.astype(bf16).astype(f32)
    lo = packed - hi
    dst[pl.ds(first, ROWS), :] = jnp.where(lane, hi, pltpu.roll(lo, 64, 1)).astype(bf16)
    dst[pl.ds(first + ROWS, ROWS), :] = jnp.where(lane, pltpu.roll(hi, 64, 1), lo).astype(bf16)


def list_pairs(todo, n, rows, row_at, cols, col_at, offset, go):
    jlo = [cols[7, j] for j in range(NB)]
    jhi = [cols[7, NB + j] for j in range(NB)]

    def row_step(i, n):
        lo = rows[7, i] - MARGIN
        hi = rows[7, NB + i] + MARGIN
        base = row_at + i + 4096 * (offset + REACH)
        for j in range(NB):
            todo[n] = base + 64 * (col_at + j)
            n = n + jnp.where((jlo[j] <= hi) & (jhi[j] >= lo), 1, 0)
        return n

    live = rows[7, LIVE_AT].astype(jnp.int32)
    if go is not None:
        live = jnp.where(go > 0.5, live, 0)
    return lax.fori_loop(0, live, row_step, n)


def run_pairs(todo, start, n, alongs, acrosses, row_meta, halves, acc):
    trash = 32
    for u in range(UNROLL):
        todo[n + u] = trash + 4096 * REACH

    def group(t, _):
        out = []
        for u in range(UNROLL):
            code = todo[start + t * UNROLL + u]
            i = code & 63
            j = (code >> 6) & 63
            shift = ((code >> 12) - REACH).astype(f32)
            im = jnp.minimum(i, trash - 1)
            ri = pl.ds(pl.multiple_of(im * BLK, BLK), BLK)
            cj = pl.ds(pl.multiple_of(j * BLK, BLK), BLK)
            da = (row_meta[0:1, cj] + shift) - alongs[ri, :]
            db = row_meta[1:2, cj] - acrosses[ri, :]
            s = jnp.minimum(jnp.maximum(da * da + db * db, 1e-30), 1.0)
            q = s * lax.rsqrt(s)
            t1 = 1.0 - q
            t2 = t1 * t1
            phi = t2 * t2 * (4.0 * q + 1.0)
            hi, lo = split(phi)
            w = halves[cj, :]
            out.append(
                (i, dot(jnp.concatenate([hi, lo], axis=1), jnp.concatenate([w, w], axis=0)))
            )
        for i, val in out:
            ro = pl.ds(pl.multiple_of(i * BLK, BLK), BLK)
            acc[ro, :] += val
        return 0

    lax.fori_loop(0, (n - start + UNROLL - 1) // UNROLL, group, 0)


def fold(acc, first):
    a = acc[pl.ds(first, ROWS), :]
    b = acc[pl.ds(first + ROWS, ROWS), :]
    lane = iota((1, 128), 1) < ENS
    return jnp.where(lane, a + pltpu.roll(a, 64, 1), b + pltpu.roll(b, 64, 1))


def flag(bounds, d):
    return bounds[7, PAIR_AT + d - 1]


def fetch_bounds(row_meta, halos, scalars, sem):
    sources = [row_meta.at[:, pl.ds(g * ROWS, BLK)] for g in range(row_meta.shape[1] // ROWS)]
    for ref in halos:
        sources += [ref.at[0, meta_rows(g * NB), :] for g in range(REACH)]
    copies = [
        pltpu.make_async_copy(src, scalars.at[k], sem.at[k]) for k, src in enumerate(sources)
    ]
    for c in copies:
        c.start()
    for c in copies:
        c.wait()
    return [scalars.at[k] for k in range(len(copies))]


def near_kernel(regions, alongs, acrosses, row_meta, wres, out, scalars, sem, todo, halves, acc):
    bounds = fetch_bounds(row_meta, [], scalars, sem)
    for p in range(regions // 2):
        load_split(halves, 2 * p * ROWS, wres[p, pl.ds(0, ROWS), :])
    acc[...] = jnp.zeros_like(acc)
    n = jnp.int32(0)
    for g in range(regions):
        for d in range(-REACH, REACH + 1):
            h = g + d
            if 0 <= h < regions:
                go = None if d == 0 else flag(bounds[min(g, h)], abs(d))
                n = list_pairs(todo, n, bounds[g], g * NB, bounds[h], h * NB, d, go)
    run_pairs(todo, 0, n, alongs, acrosses, row_meta, halves, acc)
    out[...] = acc[: regions * ROWS, :]


def far_kernel(regions, col_meta, alongs, acrosses, row_meta, pres, nres, res, part, img_out, wimg_out,
               scalars, sem, todo, halves, acc, rowm):
    bounds = fetch_bounds(row_meta, [pres, nres], scalars, sem)
    pbounds, nbounds = bounds[regions : regions + REACH], bounds[regions + REACH :]
    span = REACH * ROWS
    load_split(halves, 0, pres[0, pl.ds(0, ROWS), :])
    load_split(halves, span, nres[0, pl.ds(0, ROWS), :])
    unpack_meta(rowm, 0, pres)
    unpack_meta(rowm, REACH * NB, nres)
    acc[: regions * ROWS, :] = part[...]
    acc[regions * ROWS :, :] = jnp.zeros((BLK, 128), f32)
    n = jnp.int32(0)
    for g in range(REACH):
        for d in range(g + 1, REACH + 1):
            h = REACH + g - d
            n = list_pairs(todo, n, bounds[g], g * NB, pbounds[h], h * NB, -d, flag(pbounds[h], d))
    for k in range(REACH):
        g = regions - REACH + k
        for d in range(REACH - k, REACH + 1):
            h = g + d - regions
            n = list_pairs(todo, n, bounds[g], g * NB, nbounds[h], (REACH + h) * NB, d, flag(bounds[g], d))
    run_pairs(todo, 0, n, alongs, acrosses, rowm, halves, acc)
    lane = iota((1, 128), 1) < ENS
    for p in range(regions // 2):
        a = col_meta[pl.ds(2 * p * ROWS, ROWS), :]
        b = col_meta[pl.ds((2 * p + 1) * ROWS, ROWS), :]
        w = jnp.where(lane, a[:, 66:67], b[:, 66:67])
        e = jnp.where(lane, a[:, 67:68], b[:, 67:68])
        image = fold(acc, 2 * p * ROWS) * w + e * res[p]
        img_out[p] = image
        wimg_out[p] = image * w


def near2_kernel(regions, alongs, acrosses, row_meta, wimg, res, img, out, gram_out,
                 scalars, sem, todo, halves, acc):
    bounds = fetch_bounds(row_meta, [], scalars, sem)
    for p in range(regions // 2):
        load_split(halves, 2 * p * ROWS, wimg[p])
    acc[...] = jnp.zeros_like(acc)
    n = jnp.int32(0)
    for g in range(regions):
        n = list_pairs(todo, n, bounds[g], g * NB, bounds[g], g * NB, 0, None)
    run_pairs(todo, 0, n, alongs, acrosses, row_meta, halves, acc)
    acc[...] = acc[...] * 0.5
    n = jnp.int32(0)
    for g in range(regions):
        for d in range(1, REACH + 1):
            if g + d < regions:
                go = flag(bounds[g], d)
                n = list_pairs(todo, n, bounds[g], g * NB, bounds[g + d], (g + d) * NB, d, go)
    run_pairs(todo, 0, n, alongs, acrosses, row_meta, halves, acc)
    out[...] = acc[: regions * ROWS, :]
    lane = iota((1, 128), 1) < ENS
    gram = jnp.zeros((128, 128), f32)
    mixed = jnp.zeros((128, 128), f32)
    for p in range(regions // 2):
        r, i = res[p], img[p]
        one = jnp.where(lane, r, pltpu.roll(i, 64, 1))
        two = jnp.where(lane, pltpu.roll(r, 64, 1), i)
        for x in (one, two):
            hi, lo = split(x)
            gram = gram + dot(hi, hi, 0, 0)
            mixed = mixed + dot(hi, lo, 0, 0)
    gram = gram + mixed + jnp.transpose(mixed)
    gram_out[...] = gram


def far2_kernel(regions, col_meta, alongs, acrosses, row_meta, nres, nimg, img, part, gram, out,
                scalars, sem, todo, halves, acc, rowm):
    bounds = fetch_bounds(row_meta, [nres], scalars, sem)
    nbounds = bounds[regions:]
    load_split(halves, 0, nimg[0])
    unpack_meta(rowm, 0, nres)
    acc[: regions * ROWS, :] = part[...]
    acc[regions * ROWS :, :] = jnp.zeros((BLK, 128), f32)
    n = jnp.int32(0)
    for k in range(REACH):
        g = regions - REACH + k
        for d in range(REACH - k, REACH + 1):
            h = g + d - regions
            n = list_pairs(todo, n, bounds[g], g * NB, nbounds[h], h * NB, d, flag(bounds[g], d))
    run_pairs(todo, 0, n, alongs, acrosses, rowm, halves, acc)
    lane = iota((1, 128), 1) < ENS
    half = jnp.zeros((128, 128), f32)
    for p in range(regions // 2):
        a = col_meta[pl.ds(2 * p * ROWS, ROWS), :]
        b = col_meta[pl.ds((2 * p + 1) * ROWS, ROWS), :]
        w = jnp.where(lane, a[:, 66:67], b[:, 66:67])
        e = jnp.where(lane, a[:, 67:68], b[:, 67:68])
        ih, il = split(img[p])
        jh, jl = split(w * fold(acc, 2 * p * ROWS) + (0.5 * e) * img[p])
        half = half + dot(ih, jh, 0, 0) + dot(ih, jl, 0, 0) + dot(il, jh, 0, 0)
    out[:, 0:64] = gram[0:64, 0:64]
    out[:, 64:128] = gram[0:64, 64:128]
    out[:, 128:192] = gram[64:128, 64:128]
    out[:, 192:256] = half[0:64, 0:64] + half[64:128, 64:128]


def slot_kernel(count, row_meta, innov, img, both_out):
    g = pl.program_id(0)
    live = iota((1, ROWS), 1) < count[g]
    r = jnp.where(live, innov[...], 0.0)
    t = jnp.transpose(img[0])
    t = jnp.where(g % 2 == 0, t[:ENS, :], t[ENS:, :])
    hi, lo = split(t)
    lhs = jnp.concatenate([hi, lo], axis=0)
    rank = row_meta[4:5, :].astype(jnp.int32)
    put = jnp.where(rank == iota((ROWS, 1), 0), 1.0, 0.0).astype(bf16)
    total = dot(lhs, put)
    both_out[...] = jnp.concatenate([r, total[:ENS, :] + total[ENS:, :]], axis=0)


def column_kernel(raw, both, sums_out):
    hi, lo = split(both[...] * raw[4:5, :])
    lhs = jnp.concatenate([hi, lo], axis=0)
    owner = raw[5:6, :].astype(jnp.int32)

    @pl.when(pl.program_id(0) == 0)
    def _():
        sums_out[...] = jnp.zeros_like(sums_out)

    step = 512
    for b in range(2 * COLS_DEV // step):
        own = jnp.where(owner == iota((step, 1), 0) + b * step, 1.0, 0.0).astype(bf16)
        y = dot(lhs, own, 1, 1)
        sums_out[:, b * step : (b + 1) * step] += y[: 2 * ENS, :] + y[2 * ENS :, :]


def eliminate(pairs):
    work = [jnp.concatenate([a, b], axis=1) for a, b in pairs]
    index = iota((ENS, 2 * ENS), 0)
    for k in range(0, ENS, GROUP):
        for p in range(len(work)):
            a = work[p]
            cols = [jnp.broadcast_to(a[:, k + c : k + c + 1], a.shape) for c in range(GROUP)]
            rows = [a[k + i : k + i + 1, :] for i in range(GROUP)]
            e = [[cols[c][k + i : k + i + 1, :] for c in range(GROUP)] for i in range(GROUP)]
            inv = []
            for c in range(GROUP):
                inv.append(1.0 / e[c][c])
                for i in range(c + 1, GROUP):
                    ratio = e[i][c] * inv[c]
                    for j in range(c + 1, GROUP):
                        e[i][j] = e[i][j] - ratio * e[c][j]
                    rows[i] = rows[i] - ratio * rows[c]
            for c in reversed(range(GROUP)):
                for j in range(c + 1, GROUP):
                    rows[c] = rows[c] - e[c][j] * rows[j]
                rows[c] = rows[c] * inv[c]
            for c in range(GROUP):
                a = a - cols[c] * rows[c]
            for c in range(GROUP):
                a = jnp.where(index == k + c, rows[c], a)
            work[p] = a
    return [a[:, ENS:] for a in work]


def finish_kernel(gram, both, sums, carried, weights_out, incr_out):
    g = gram[...]
    hd = functools.partial(dot, precision=highest)

    def sym(a):
        return 0.5 * (a + jnp.transpose(a))

    n0 = sym(g[:, 0:64])
    k0 = sym(g[:, 64:128])
    m0 = sym(g[:, 128:192])
    l0 = g[:, 192:256] + jnp.transpose(g[:, 192:256])
    eye = jnp.where(iota((ENS, ENS), 0) == iota((ENS, ENS), 1), 1.0, 0.0)
    s0, inv = eliminate([(k0, n0), (n0, eye)])
    s0t = jnp.transpose(s0)
    ks = hd(k0, s0)
    ms = hd(m0, s0)
    n1 = sym(n0 - ks - jnp.transpose(ks) + hd(s0t, ms))
    b = eye + hd(inv, n1)
    bt = jnp.transpose(b)
    cross = hd(bt, ms)
    c1 = sym(hd(bt, hd(k0, b)) - cross - jnp.transpose(cross) + hd(s0t, hd(l0, s0)))
    (s1,) = eliminate([(c1, n1)])
    mix = jnp.concatenate([s0 + hd(b, s1), -hd(s0, s1)], axis=0)
    mt = jnp.transpose(mix)
    hi, lo = split(mt)
    lhs = jnp.concatenate([hi, hi, lo], axis=1)

    def apply(x):
        xh, xl = split(x)
        return dot(lhs, jnp.concatenate([xh, xl, xh], axis=0))

    step = 512
    for c in range(weights_out.shape[1] // step):
        at = pl.ds(c * step, step)
        weights_out[:, at] = apply(both[:, at])
    for c in range(COLS_DEV // step):
        at = pl.ds(c * step, step)
        incr_out[:, at] = apply(sums[:, at] + carried[:, at])


def on_device(innovation, obs_along, obs_across, obs_scale, obs_error, obs_gain, pair_live, obs_count, col_owner):
    regions = obs_count.shape[0]
    local = regions * ROWS
    packs = regions // 2
    span = REACH * ROWS
    total_cols = COLS_DEV * lax.axis_size(AXES)
    owner = (col_owner - lax.axis_index(AXES) * COLS_DEV) % total_cols
    zero = jnp.zeros((local,), f32)
    raw = jnp.stack(
        [obs_along, obs_across, obs_scale, obs_error, obs_gain, owner.astype(f32), zero, zero]
    )
    shape = jax.ShapeDtypeStruct
    packed = shape((packs, ROWS, 128), f32)
    row_spec = pl.BlockSpec((8, ROWS), lambda g: (0, g))
    pack_spec = pl.BlockSpec((1, ROWS, 128), lambda g: (g // 2, 0, 0))
    held = ROWS + 16 * NB
    held_spec = pl.BlockSpec((1, held, 128), lambda g: (g // 2, 0, 0))
    member_spec = pl.BlockSpec((ENS, ROWS), lambda g: (0, g))
    row_meta, col_meta, alongs, acrosses, res, wres = pl.pallas_call(
        sort_kernel,
        grid=(regions,),
        in_specs=[SMEM, SMEM, row_spec, member_spec],
        out_specs=[row_spec] + [pl.BlockSpec((ROWS, 128), lambda g: (g, 0))] * 3 + [pack_spec, held_spec],
        out_shape=[shape((8, local), f32)] + [shape((local, 128), f32)] * 3 + [packed, shape((packs, held, 128), f32)],
        compiler_params=params(24),
        name="order",
    )(obs_count, pair_live, raw, innovation)

    pres = from_behind(wres[packs - 1 :], 1)
    nres = from_behind(wres[:1], -1)
    def scratch(blocks):
        halos = regions + 2 * REACH
        return [
            pltpu.SMEM((halos, 8, BLK), f32),
            pltpu.SemaphoreType.DMA((halos,)),
            pltpu.SMEM((20 * 64 + 8,), jnp.int32),
            pltpu.VMEM((blocks * ROWS, 128), bf16),
            pltpu.VMEM((local + BLK, 128), f32),
        ]

    plain = shape((local, 128), f32)

    part = pl.pallas_call(
        functools.partial(near_kernel, regions),
        in_specs=[VMEM] * 4,
        out_specs=VMEM,
        out_shape=plain,
        scratch_shapes=scratch(regions),
        compiler_params=params(24),
        cost_estimate=cost(int(4e9), int(2e7)),
        name="near",
    )(alongs, acrosses, row_meta, wres)
    img, wimg = pl.pallas_call(
        functools.partial(far_kernel, regions),
        in_specs=[VMEM] * 8,
        out_specs=[VMEM, VMEM],
        out_shape=[packed, packed],
        scratch_shapes=scratch(2 * REACH) + [pltpu.VMEM((8, 2 * span), f32)],
        compiler_params=params(24),
        name="far",
    )(col_meta, alongs, acrosses, row_meta, pres, nres, res, part)
    nimg = from_behind(wimg[:1], -1)
    part2, gram = pl.pallas_call(
        functools.partial(near2_kernel, regions),
        in_specs=[VMEM] * 6,
        out_specs=[VMEM, VMEM],
        out_shape=[plain, shape((128, 128), f32)],
        scratch_shapes=scratch(regions),
        compiler_params=params(24),
        cost_estimate=cost(int(4e9), int(2e7)),
        name="near_again",
    )(alongs, acrosses, row_meta, wimg, res, img)
    gram = pl.pallas_call(
        functools.partial(far2_kernel, regions),
        in_specs=[VMEM] * 9,
        out_specs=VMEM,
        out_shape=shape((ENS, 4 * ENS), f32),
        scratch_shapes=scratch(REACH) + [pltpu.VMEM((8, span), f32)],
        compiler_params=params(24),
        name="far_again",
    )(col_meta, alongs, acrosses, row_meta, nres, nimg, img, part2, gram)

    both_spec = pl.BlockSpec((2 * ENS, ROWS), lambda g: (0, g))
    both = pl.pallas_call(
        slot_kernel,
        grid=(regions,),
        in_specs=[SMEM, row_spec, member_spec, pack_spec],
        out_specs=both_spec,
        out_shape=shape((2 * ENS, local), f32),
        compiler_params=params(24),
        cost_estimate=cost(int(4e9), int(1e7)),
        name="slots",
    )(obs_count, row_meta, innovation, img)

    def columns(values):
        return pl.pallas_call(
            column_kernel,
            grid=(regions,),
            in_specs=[row_spec, both_spec],
            out_specs=pl.BlockSpec((2 * ENS, 2 * COLS_DEV), lambda g: (0, 0)),
            out_shape=shape((2 * ENS, 2 * COLS_DEV), f32),
            compiler_params=params(24),
            cost_estimate=cost(int(4e9), int(1e7)),
            name="columns",
        )(raw, values)

    gram, both, sums = all_sum(gram, both, columns)
    carried = from_behind(sums[:, COLS_DEV:], 1)
    return tuple(
        pl.pallas_call(
            finish_kernel,
            in_specs=[VMEM] * 4,
            out_specs=[VMEM, VMEM],
            out_shape=[shape((ENS, local), f32), shape((ENS, COLS_DEV), f32)],
            compiler_params=params(24),
            name="finish",
        )(gram, both, sums, carried)
    )


def solution(mesh):
    row = P(None, AXES)
    vec = P(AXES)
    in_specs = (row, vec, vec, vec, vec, vec, P(AXES, None), vec, vec)
    return jax.shard_map(
        on_device, mesh=mesh, in_specs=in_specs, out_specs=(row, row), check_vma=False
    )
```

```python
import functools

import jax
import jax.numpy as jnp
from jax import lax
from jax.experimental import pallas as pl
from jax.experimental.pallas import tpu as pltpu
from jax.sharding import PartitionSpec as P

ROWS = 1024
REACH = 2
ENS = 64
BLK = 128
NB = ROWS // BLK
COLS_DEV = 1024
AXES = ("reg", "col")
FAR = 40.0
TOP = 32.0
MARGIN = 1.0001
PAIR_AT = 2 * NB
LIVE_AT = PAIR_AT + REACH
UNROLL = 16
GROUP = 8
f32 = jnp.float32
bf16 = jnp.bfloat16
highest = lax.Precision.HIGHEST


def from_behind(block, distance):
    size = lax.axis_size(AXES)
    return lax.ppermute(block, AXES, [((i - distance) % size, i) for i in range(size)])


def turned(block, stride, length, by):
    size = lax.axis_size(AXES)
    route = []
    for i in range(size):
        place = (i // stride) % length
        route.append((i, i + ((place + by) % length - place) * stride))
    return lax.ppermute(block, AXES, route)


def all_sum(block, beside, make):
    size = lax.axis_size(AXES)
    stride = 1
    made = None
    while stride < size:
        length = 2 if stride == 1 else min(4, size // stride)
        if stride > 1 and made is None:
            block, beside = lax.optimization_barrier((block, beside))
            made = make(beside)
        elif made is not None:
            both, sums, carried = made
            if carried is None:
                block, sums = lax.optimization_barrier((block, sums))
                carried = from_behind(sums[:, COLS_DEV:], 1)
            else:
                block, carried = lax.optimization_barrier((block, carried))
            made = both, sums, carried
        if length == 2:
            block = block + turned(block, stride, 2, 1)
        else:
            one = turned(block, stride, 4, 1)
            two = turned(block, stride, 4, 2)
            three = turned(block, stride, 4, 3)
            block = (block + two) + (one + three)
        stride *= length
    both, sums, carried = make(beside) if made is None else made
    if carried is None:
        carried = from_behind(sums[:, COLS_DEV:], 1)
    return block, both, sums, carried


def dot(a, b, ca=1, cb=0, precision=None):
    return lax.dot_general(
        a, b, (((ca,), (cb,)), ((), ())), precision=precision, preferred_element_type=f32
    )


def iota(shape, dim):
    return lax.broadcasted_iota(jnp.int32, shape, dim)


def split(x):
    hi = x.astype(bf16)
    return hi, (x - hi.astype(f32)).astype(bf16)


def params(mib, **kw):
    return pltpu.CompilerParams(vmem_limit_bytes=mib << 20, **kw)


def cost(flops, moved):
    return pl.CostEstimate(flops=flops, bytes_accessed=moved, transcendentals=0)


SMEM = pl.BlockSpec(memory_space=pltpu.SMEM)
VMEM = pl.BlockSpec(memory_space=pltpu.VMEM)


def sort_kernel(count, pair, meta, innov, row_out, col_out, along_out, across_out, res_out, wres_out):
    g = pl.program_id(0)
    idx = iota((1, ROWS), 1)
    live = idx < count[g]
    along, scale, err = meta[0:1, :], meta[2:3, :], meta[3:4, :]
    key = jnp.where(live, meta[1:2, :], FAR)
    key_col = jnp.transpose(jnp.broadcast_to(key, (8, ROWS)))
    rank = jnp.zeros((1, ROWS), f32)
    for b in range(NB):
        kc = key_col[b * BLK : (b + 1) * BLK, 0:1]
        at, end = b * BLK, (b + 1) * BLK
        here = key[:, at:end]
        tie = (kc == here) & (iota((BLK, BLK), 0) < iota((BLK, BLK), 1))
        counted = [jnp.where((kc < here) | tie, 1.0, 0.0)]
        if at > 0:
            counted.insert(0, jnp.where(kc < key[:, :at], 1.0, 0.0))
        if end < ROWS:
            counted.append(jnp.where(kc <= key[:, end:], 1.0, 0.0))
        rank = rank + jnp.concatenate(
            [jnp.sum(x, axis=0, keepdims=True) for x in counted], axis=1
        )
    rank = rank.astype(jnp.int32)
    x = jnp.where(live, innov[...], 0.0)
    quarter = jnp.where(live, scale * 0.25, 0.0)
    m = jnp.concatenate([along, key, quarter, err], axis=0)
    xh, xr = x.astype(bf16), x - x.astype(bf16).astype(f32)
    xm, xl = split(xr)
    mh, mr = m.astype(bf16).astype(f32), m - m.astype(bf16).astype(f32)
    mm = mr.astype(bf16).astype(f32)
    ml = mr - mm
    metas = jnp.concatenate([mh, mm, ml, jnp.zeros((52, ROWS), f32)], axis=0).astype(bf16)
    data = jnp.concatenate([xh, xm, xl, metas], axis=0)
    pick = jnp.where(rank == iota((ROWS, 1), 0), 1.0, 0.0).astype(bf16)
    ordered = dot(pick, data, 1, 1)
    step = 256
    for b in range(ROWS // step):
        y = ordered[b * step : (b + 1) * step, :]
        t0, t1 = y[:, :128], y[:, 128:]
        r = t0 + pltpu.roll(t0, 64, 1) + t1
        c = t1 + pltpu.roll(t1, 124, 1) + pltpu.roll(t1, 120, 1)
        rows = pl.ds(b * step, step)
        col_out[rows, :] = c
        along_out[rows, :] = jnp.broadcast_to(c[:, 64:65], (step, 128))
        across_out[rows, :] = jnp.broadcast_to(c[:, 65:66], (step, 128))
        u = r * c[:, 66:67]
        for s in range(2):

            @pl.when(g % 2 == s)
            def _(s=s, r=r, u=u, rows=rows):
                res_out[0, rows, s * ENS : (s + 1) * ENS] = r[:, :ENS]
                wres_out[0, rows, s * ENS : (s + 1) * ENS] = u[:, :ENS]

        row_out[0:4, rows] = jnp.transpose(c)[64:68, :]
    row_out[4:5, :] = rank.astype(f32)
    lane = iota((1, ROWS), 1)
    bound = jnp.where(lane == PAIR_AT, pair[g, 0], jnp.where(lane == PAIR_AT + 1, pair[g, 1], 0))
    bound = bound.astype(f32)
    bound = jnp.where(lane == LIVE_AT, ((count[g] + BLK - 1) // BLK).astype(f32), bound)
    for b in range(NB):
        first = row_out[1:2, b * BLK : b * BLK + 1]
        last = row_out[1:2, (b + 1) * BLK - 1 : (b + 1) * BLK]
        bound = jnp.where(lane == b, first, bound)
        bound = jnp.where(lane == NB + b, jnp.minimum(last, TOP), bound)
    row_out[5:8, :] = jnp.broadcast_to(bound, (3, ROWS))
    for s in range(2):

        @pl.when(g % 2 == s)
        def _(s=s):
            for b in range(NB):
                wres_out[0, meta_rows(s * NB + b), :] = row_out[:, b * BLK : (b + 1) * BLK]


def meta_rows(block):
    return pl.ds(ROWS + 8 * block, 8)


def unpack_meta(dst, first, packed):
    for b in range(2 * NB):
        dst[:, pl.ds((first + b) * BLK, BLK)] = packed[0, meta_rows(b), :]


def load_split(dst, first, packed):
    lane = iota((1, 128), 1) < ENS
    hi = packed.astype(bf16).astype(f32)
    lo = packed - hi
    dst[pl.ds(first, ROWS), :] = jnp.where(lane, hi, pltpu.roll(lo, 64, 1)).astype(bf16)
    dst[pl.ds(first + ROWS, ROWS), :] = jnp.where(lane, pltpu.roll(hi, 64, 1), lo).astype(bf16)


def list_pairs(todo, n, rows, row_at, cols, col_at, offset, go):
    jlo = [cols[7, j] for j in range(NB)]
    jhi = [cols[7, NB + j] for j in range(NB)]

    def row_step(i, n):
        lo = rows[7, i] - MARGIN
        hi = rows[7, NB + i] + MARGIN
        base = row_at + i + 4096 * (offset + REACH)
        for j in range(NB):
            todo[n] = base + 64 * (col_at + j)
            n = n + jnp.where((jlo[j] <= hi) & (jhi[j] >= lo), 1, 0)
        return n

    live = rows[7, LIVE_AT].astype(jnp.int32)
    if go is not None:
        live = jnp.where(go > 0.5, live, 0)
    return lax.fori_loop(0, live, row_step, n)


def run_pairs(todo, start, n, alongs, acrosses, row_meta, halves, acc):
    trash = 32
    for u in range(UNROLL):
        todo[n + u] = trash + 4096 * REACH

    def group(t, _):
        out = []
        for u in range(UNROLL):
            code = todo[start + t * UNROLL + u]
            i = code & 63
            j = (code >> 6) & 63
            shift = ((code >> 12) - REACH).astype(f32)
            im = jnp.minimum(i, trash - 1)
            ri = pl.ds(pl.multiple_of(im * BLK, BLK), BLK)
            cj = pl.ds(pl.multiple_of(j * BLK, BLK), BLK)
            da = (row_meta[0:1, cj] + shift) - alongs[ri, :]
            db = row_meta[1:2, cj] - acrosses[ri, :]
            s = jnp.minimum(jnp.maximum(da * da + db * db, 1e-30), 1.0)
            q = s * lax.rsqrt(s)
            t1 = 1.0 - q
            t2 = t1 * t1
            phi = t2 * t2 * (4.0 * q + 1.0)
            hi, lo = split(phi)
            w = halves[cj, :]
            out.append(
                (i, dot(jnp.concatenate([hi, lo], axis=1), jnp.concatenate([w, w], axis=0)))
            )
        for i, val in out:
            ro = pl.ds(pl.multiple_of(i * BLK, BLK), BLK)
            acc[ro, :] += val
        return 0

    lax.fori_loop(0, (n - start + UNROLL - 1) // UNROLL, group, 0)


def fold(acc, first):
    a = acc[pl.ds(first, ROWS), :]
    b = acc[pl.ds(first + ROWS, ROWS), :]
    lane = iota((1, 128), 1) < ENS
    return jnp.where(lane, a + pltpu.roll(a, 64, 1), b + pltpu.roll(b, 64, 1))


def flag(bounds, d):
    return bounds[7, PAIR_AT + d - 1]


def fetch_bounds(row_meta, halos, scalars, sem):
    sources = [row_meta.at[:, pl.ds(g * ROWS, BLK)] for g in range(row_meta.shape[1] // ROWS)]
    for ref in halos:
        sources += [ref.at[0, meta_rows(g * NB), :] for g in range(REACH)]
    copies = [
        pltpu.make_async_copy(src, scalars.at[k], sem.at[k]) for k, src in enumerate(sources)
    ]
    for c in copies:
        c.start()
    for c in copies:
        c.wait()
    return [scalars.at[k] for k in range(len(copies))]


def near_kernel(regions, alongs, acrosses, row_meta, wres, out, scalars, sem, todo, halves, acc):
    bounds = fetch_bounds(row_meta, [], scalars, sem)
    for p in range(regions // 2):
        load_split(halves, 2 * p * ROWS, wres[p, pl.ds(0, ROWS), :])
    acc[...] = jnp.zeros_like(acc)
    n = jnp.int32(0)
    for g in range(regions):
        for d in range(-REACH, REACH + 1):
            h = g + d
            if 0 <= h < regions:
                go = None if d == 0 else flag(bounds[min(g, h)], abs(d))
                n = list_pairs(todo, n, bounds[g], g * NB, bounds[h], h * NB, d, go)
    run_pairs(todo, 0, n, alongs, acrosses, row_meta, halves, acc)
    out[...] = acc[: regions * ROWS, :]


def far_kernel(regions, col_meta, alongs, acrosses, row_meta, pres, nres, res, part, img_out, wimg_out,
               scalars, sem, todo, halves, acc, rowm):
    bounds = fetch_bounds(row_meta, [pres, nres], scalars, sem)
    pbounds, nbounds = bounds[regions : regions + REACH], bounds[regions + REACH :]
    span = REACH * ROWS
    load_split(halves, 0, pres[0, pl.ds(0, ROWS), :])
    load_split(halves, span, nres[0, pl.ds(0, ROWS), :])
    unpack_meta(rowm, 0, pres)
    unpack_meta(rowm, REACH * NB, nres)
    acc[: regions * ROWS, :] = part[...]
    acc[regions * ROWS :, :] = jnp.zeros((BLK, 128), f32)
    n = jnp.int32(0)
    for g in range(REACH):
        for d in range(g + 1, REACH + 1):
            h = REACH + g - d
            n = list_pairs(todo, n, bounds[g], g * NB, pbounds[h], h * NB, -d, flag(pbounds[h], d))
    for k in range(REACH):
        g = regions - REACH + k
        for d in range(REACH - k, REACH + 1):
            h = g + d - regions
            n = list_pairs(todo, n, bounds[g], g * NB, nbounds[h], (REACH + h) * NB, d, flag(bounds[g], d))
    run_pairs(todo, 0, n, alongs, acrosses, rowm, halves, acc)
    lane = iota((1, 128), 1) < ENS
    for p in range(regions // 2):
        a = col_meta[pl.ds(2 * p * ROWS, ROWS), :]
        b = col_meta[pl.ds((2 * p + 1) * ROWS, ROWS), :]
        w = jnp.where(lane, a[:, 66:67], b[:, 66:67])
        e = jnp.where(lane, a[:, 67:68], b[:, 67:68])
        image = fold(acc, 2 * p * ROWS) * w + e * res[p]
        img_out[p] = image
        wimg_out[p] = image * w


def near2_kernel(regions, alongs, acrosses, row_meta, wimg, res, img, out, gram_out,
                 scalars, sem, todo, halves, acc):
    bounds = fetch_bounds(row_meta, [], scalars, sem)
    for p in range(regions // 2):
        load_split(halves, 2 * p * ROWS, wimg[p])
    acc[...] = jnp.zeros_like(acc)
    n = jnp.int32(0)
    for g in range(regions):
        n = list_pairs(todo, n, bounds[g], g * NB, bounds[g], g * NB, 0, None)
    run_pairs(todo, 0, n, alongs, acrosses, row_meta, halves, acc)
    acc[...] = acc[...] * 0.5
    n = jnp.int32(0)
    for g in range(regions):
        for d in range(1, REACH + 1):
            if g + d < regions:
                go = flag(bounds[g], d)
                n = list_pairs(todo, n, bounds[g], g * NB, bounds[g + d], (g + d) * NB, d, go)
    run_pairs(todo, 0, n, alongs, acrosses, row_meta, halves, acc)
    out[...] = acc[: regions * ROWS, :]
    lane = iota((1, 128), 1) < ENS
    gram = jnp.zeros((128, 128), f32)
    mixed = jnp.zeros((128, 128), f32)
    for p in range(regions // 2):
        r, i = res[p], img[p]
        one = jnp.where(lane, r, pltpu.roll(i, 64, 1))
        two = jnp.where(lane, pltpu.roll(r, 64, 1), i)
        for x in (one, two):
            hi, lo = split(x)
            gram = gram + dot(hi, hi, 0, 0)
            mixed = mixed + dot(hi, lo, 0, 0)
    gram = gram + mixed + jnp.transpose(mixed)
    gram_out[...] = gram


def far2_kernel(regions, col_meta, alongs, acrosses, row_meta, nres, nimg, img, part, gram, out,
                scalars, sem, todo, halves, acc, rowm):
    bounds = fetch_bounds(row_meta, [nres], scalars, sem)
    nbounds = bounds[regions:]
    load_split(halves, 0, nimg[0])
    unpack_meta(rowm, 0, nres)
    acc[: regions * ROWS, :] = part[...]
    acc[regions * ROWS :, :] = jnp.zeros((BLK, 128), f32)
    n = jnp.int32(0)
    for k in range(REACH):
        g = regions - REACH + k
        for d in range(REACH - k, REACH + 1):
            h = g + d - regions
            n = list_pairs(todo, n, bounds[g], g * NB, nbounds[h], h * NB, d, flag(bounds[g], d))
    run_pairs(todo, 0, n, alongs, acrosses, rowm, halves, acc)
    lane = iota((1, 128), 1) < ENS
    half = jnp.zeros((128, 128), f32)
    for p in range(regions // 2):
        a = col_meta[pl.ds(2 * p * ROWS, ROWS), :]
        b = col_meta[pl.ds((2 * p + 1) * ROWS, ROWS), :]
        w = jnp.where(lane, a[:, 66:67], b[:, 66:67])
        e = jnp.where(lane, a[:, 67:68], b[:, 67:68])
        ih, il = split(img[p])
        jh, jl = split(w * fold(acc, 2 * p * ROWS) + (0.5 * e) * img[p])
        half = half + dot(ih, jh, 0, 0) + dot(ih, jl, 0, 0) + dot(il, jh, 0, 0)
    out[:, 0:64] = gram[0:64, 0:64]
    out[:, 64:128] = gram[0:64, 64:128]
    out[:, 128:192] = gram[64:128, 64:128]
    out[:, 192:256] = half[0:64, 0:64] + half[64:128, 64:128]


def slot_kernel(count, row_meta, innov, img, both_out):
    g = pl.program_id(0)
    live = iota((1, ROWS), 1) < count[g]
    r = jnp.where(live, innov[...], 0.0)
    t = jnp.transpose(img[0])
    t = jnp.where(g % 2 == 0, t[:ENS, :], t[ENS:, :])
    hi, lo = split(t)
    lhs = jnp.concatenate([hi, lo], axis=0)
    rank = row_meta[4:5, :].astype(jnp.int32)
    put = jnp.where(rank == iota((ROWS, 1), 0), 1.0, 0.0).astype(bf16)
    total = dot(lhs, put)
    both_out[...] = jnp.concatenate([r, total[:ENS, :] + total[ENS:, :]], axis=0)


def column_kernel(raw, both, sums_out):
    hi, lo = split(both[...] * raw[4:5, :])
    lhs = jnp.concatenate([hi, lo], axis=0)
    owner = raw[5:6, :].astype(jnp.int32)

    @pl.when(pl.program_id(0) == 0)
    def _():
        sums_out[...] = jnp.zeros_like(sums_out)

    step = 512
    for b in range(2 * COLS_DEV // step):
        own = jnp.where(owner == iota((step, 1), 0) + b * step, 1.0, 0.0).astype(bf16)
        y = dot(lhs, own, 1, 1)
        sums_out[:, b * step : (b + 1) * step] += y[: 2 * ENS, :] + y[2 * ENS :, :]


def eliminate(pairs):
    work = [jnp.concatenate([a, b], axis=1) for a, b in pairs]
    index = iota((ENS, 2 * ENS), 0)
    for k in range(0, ENS, GROUP):
        for p in range(len(work)):
            a = work[p]
            cols = [jnp.broadcast_to(a[:, k + c : k + c + 1], a.shape) for c in range(GROUP)]
            rows = [a[k + i : k + i + 1, :] for i in range(GROUP)]
            e = [[cols[c][k + i : k + i + 1, :] for c in range(GROUP)] for i in range(GROUP)]
            inv = []
            for c in range(GROUP):
                inv.append(1.0 / e[c][c])
                for i in range(c + 1, GROUP):
                    ratio = e[i][c] * inv[c]
                    for j in range(c + 1, GROUP):
                        e[i][j] = e[i][j] - ratio * e[c][j]
                    rows[i] = rows[i] - ratio * rows[c]
            for c in reversed(range(GROUP)):
                for j in range(c + 1, GROUP):
                    rows[c] = rows[c] - e[c][j] * rows[j]
                rows[c] = rows[c] * inv[c]
            for c in range(GROUP):
                a = a - cols[c] * rows[c]
            for c in range(GROUP):
                a = jnp.where(index == k + c, rows[c], a)
            work[p] = a
    return [a[:, ENS:] for a in work]


def finish_kernel(gram, both, sums, carried, weights_out, incr_out):
    g = gram[...]
    hd = functools.partial(dot, precision=highest)

    def sym(a):
        return 0.5 * (a + jnp.transpose(a))

    n0 = sym(g[:, 0:64])
    k0 = sym(g[:, 64:128])
    m0 = sym(g[:, 128:192])
    l0 = g[:, 192:256] + jnp.transpose(g[:, 192:256])
    eye = jnp.where(iota((ENS, ENS), 0) == iota((ENS, ENS), 1), 1.0, 0.0)
    s0, inv = eliminate([(k0, n0), (n0, eye)])
    s0t = jnp.transpose(s0)
    ks = hd(k0, s0)
    ms = hd(m0, s0)
    n1 = sym(n0 - ks - jnp.transpose(ks) + hd(s0t, ms))
    b = eye + hd(inv, n1)
    bt = jnp.transpose(b)
    cross = hd(bt, ms)
    c1 = sym(hd(bt, hd(k0, b)) - cross - jnp.transpose(cross) + hd(s0t, hd(l0, s0)))
    (s1,) = eliminate([(c1, n1)])
    mix = jnp.concatenate([s0 + hd(b, s1), -hd(s0, s1)], axis=0)
    mt = jnp.transpose(mix)
    hi, lo = split(mt)
    lhs = jnp.concatenate([hi, hi, lo], axis=1)

    def apply(x):
        xh, xl = split(x)
        return dot(lhs, jnp.concatenate([xh, xl, xh], axis=0))

    step = 512
    for c in range(weights_out.shape[1] // step):
        at = pl.ds(c * step, step)
        weights_out[:, at] = apply(both[:, at])
    for c in range(COLS_DEV // step):
        at = pl.ds(c * step, step)
        incr_out[:, at] = apply(sums[:, at] + carried[:, at])


def on_device(innovation, obs_along, obs_across, obs_scale, obs_error, obs_gain, pair_live, obs_count, col_owner):
    regions = obs_count.shape[0]
    local = regions * ROWS
    packs = regions // 2
    span = REACH * ROWS
    total_cols = COLS_DEV * lax.axis_size(AXES)
    owner = col_owner - lax.axis_index(AXES) * COLS_DEV
    owner = jnp.where(owner < 0, owner + total_cols, owner)
    zero = jnp.zeros((local,), f32)
    raw = jnp.stack(
        [obs_along, obs_across, obs_scale, obs_error, obs_gain, owner.astype(f32), zero, zero]
    )
    shape = jax.ShapeDtypeStruct
    packed = shape((packs, ROWS, 128), f32)
    row_spec = pl.BlockSpec((8, ROWS), lambda g: (0, g))
    pack_spec = pl.BlockSpec((1, ROWS, 128), lambda g: (g // 2, 0, 0))
    held = ROWS + 16 * NB
    held_spec = pl.BlockSpec((1, held, 128), lambda g: (g // 2, 0, 0))
    member_spec = pl.BlockSpec((ENS, ROWS), lambda g: (0, g))
    row_meta, col_meta, alongs, acrosses, res, wres = pl.pallas_call(
        sort_kernel,
        grid=(regions,),
        in_specs=[SMEM, SMEM, row_spec, member_spec],
        out_specs=[row_spec] + [pl.BlockSpec((ROWS, 128), lambda g: (g, 0))] * 3 + [pack_spec, held_spec],
        out_shape=[shape((8, local), f32)] + [shape((local, 128), f32)] * 3 + [packed, shape((packs, held, 128), f32)],
        compiler_params=params(24),
        name="order",
    )(obs_count, pair_live, raw, innovation)

    pres = from_behind(wres[packs - 1 :], 1)
    nres = from_behind(wres[:1], -1)
    def scratch(blocks):
        halos = regions + 2 * REACH
        return [
            pltpu.SMEM((halos, 8, BLK), f32),
            pltpu.SemaphoreType.DMA((halos,)),
            pltpu.SMEM((20 * 64 + 8,), jnp.int32),
            pltpu.VMEM((blocks * ROWS, 128), bf16),
            pltpu.VMEM((local + BLK, 128), f32),
        ]

    plain = shape((local, 128), f32)

    part = pl.pallas_call(
        functools.partial(near_kernel, regions),
        in_specs=[VMEM] * 4,
        out_specs=VMEM,
        out_shape=plain,
        scratch_shapes=scratch(regions),
        compiler_params=params(24),
        cost_estimate=cost(int(4e9), int(2e7)),
        name="near",
    )(alongs, acrosses, row_meta, wres)
    img, wimg = pl.pallas_call(
        functools.partial(far_kernel, regions),
        in_specs=[VMEM] * 8,
        out_specs=[VMEM, VMEM],
        out_shape=[packed, packed],
        scratch_shapes=scratch(2 * REACH) + [pltpu.VMEM((8, 2 * span), f32)],
        compiler_params=params(24),
        name="far",
    )(col_meta, alongs, acrosses, row_meta, pres, nres, res, part)
    nimg = from_behind(wimg[:1], -1)
    part2, gram = pl.pallas_call(
        functools.partial(near2_kernel, regions),
        in_specs=[VMEM] * 6,
        out_specs=[VMEM, VMEM],
        out_shape=[plain, shape((128, 128), f32)],
        scratch_shapes=scratch(regions),
        compiler_params=params(24),
        cost_estimate=cost(int(4e9), int(2e7)),
        name="near_again",
    )(alongs, acrosses, row_meta, wimg, res, img)
    gram = pl.pallas_call(
        functools.partial(far2_kernel, regions),
        in_specs=[VMEM] * 9,
        out_specs=VMEM,
        out_shape=shape((ENS, 4 * ENS), f32),
        scratch_shapes=scratch(REACH) + [pltpu.VMEM((8, span), f32)],
        compiler_params=params(24),
        name="far_again",
    )(col_meta, alongs, acrosses, row_meta, nres, nimg, img, part2, gram)

    both_spec = pl.BlockSpec((2 * ENS, ROWS), lambda g: (0, g))
    def columns(image):
        values = pl.pallas_call(
            slot_kernel,
            grid=(regions,),
            in_specs=[SMEM, row_spec, member_spec, pack_spec],
            out_specs=both_spec,
            out_shape=shape((2 * ENS, local), f32),
            compiler_params=params(24),
            cost_estimate=cost(int(4e9), int(1e7)),
            name="slots",
        )(obs_count, row_meta, innovation, image)
        sums = pl.pallas_call(
            column_kernel,
            grid=(regions,),
            in_specs=[row_spec, both_spec],
            out_specs=pl.BlockSpec((2 * ENS, 2 * COLS_DEV), lambda g: (0, 0)),
            out_shape=shape((2 * ENS, 2 * COLS_DEV), f32),
            compiler_params=params(24),
            cost_estimate=cost(int(4e9), int(1e7)),
            name="columns",
        )(raw, values)
        return values, sums, None

    gram, both, sums, carried = all_sum(gram, img, columns)
    return tuple(
        pl.pallas_call(
            finish_kernel,
            in_specs=[VMEM] * 4,
            out_specs=[VMEM, VMEM],
            out_shape=[shape((ENS, local), f32), shape((ENS, COLS_DEV), f32)],
            compiler_params=params(24),
            name="finish",
        )(gram, both, sums, carried)
    )


def solution(mesh):
    row = P(None, AXES)
    vec = P(AXES)
    in_specs = (row, vec, vec, vec, vec, vec, P(AXES, None), vec, vec)
    return jax.shard_map(
        on_device, mesh=mesh, in_specs=in_specs, out_specs=(row, row), check_vma=False
    )
```

```python
import functools

import jax
import jax.numpy as jnp
from jax import lax
from jax.experimental import pallas as pl
from jax.experimental.pallas import tpu as pltpu
from jax.sharding import PartitionSpec as P

ROWS = 1024
REACH = 2
ENS = 64
BLK = 128
NB = ROWS // BLK
COLS_DEV = 1024
AXES = ("reg", "col")
FAR = 40.0
TOP = 32.0
MARGIN = 1.0001
PAIR_AT = 2 * NB
LIVE_AT = PAIR_AT + REACH
UNROLL = 16
GROUP = 8
f32 = jnp.float32
bf16 = jnp.bfloat16
highest = lax.Precision.HIGHEST


def from_behind(block, distance):
    size = lax.axis_size(AXES)
    return lax.ppermute(block, AXES, [((i - distance) % size, i) for i in range(size)])


def turned(block, stride, length, by):
    size = lax.axis_size(AXES)
    route = []
    for i in range(size):
        place = (i // stride) % length
        route.append((i, i + ((place + by) % length - place) * stride))
    return lax.ppermute(block, AXES, route)


def all_sum(block, beside, make):
    size = lax.axis_size(AXES)
    stride = 1
    made = None
    while stride < size:
        length = 2 if stride == 1 else min(4, size // stride)
        if stride > 2 and made is None:
            made = make(beside)
        if length == 2:
            block = block + turned(block, stride, 2, 1)
        else:
            one = turned(block, stride, 4, 1)
            two = turned(block, stride, 4, 2)
            three = turned(block, stride, 4, 3)
            block = (block + two) + (one + three)
        stride *= length
    return block, beside, make(beside) if made is None else made


def dot(a, b, ca=1, cb=0, precision=None):
    return lax.dot_general(
        a, b, (((ca,), (cb,)), ((), ())), precision=precision, preferred_element_type=f32
    )


def iota(shape, dim):
    return lax.broadcasted_iota(jnp.int32, shape, dim)


def split(x):
    hi = x.astype(bf16)
    return hi, (x - hi.astype(f32)).astype(bf16)


def params(mib, **kw):
    return pltpu.CompilerParams(vmem_limit_bytes=mib << 20, **kw)


def cost(flops, moved):
    return pl.CostEstimate(flops=flops, bytes_accessed=moved, transcendentals=0)


SMEM = pl.BlockSpec(memory_space=pltpu.SMEM)
VMEM = pl.BlockSpec(memory_space=pltpu.VMEM)


def sort_kernel(count, pair, meta, innov, row_out, col_out, along_out, across_out, res_out, wres_out):
    g = pl.program_id(0)
    idx = iota((1, ROWS), 1)
    live = idx < count[g]
    along, scale, err = meta[0:1, :], meta[2:3, :], meta[3:4, :]
    key = jnp.where(live, meta[1:2, :], FAR)
    key_col = jnp.transpose(jnp.broadcast_to(key, (8, ROWS)))
    rank = jnp.zeros((1, ROWS), f32)
    for b in range(NB):
        kc = key_col[b * BLK : (b + 1) * BLK, 0:1]
        at, end = b * BLK, (b + 1) * BLK
        here = key[:, at:end]
        tie = (kc == here) & (iota((BLK, BLK), 0) < iota((BLK, BLK), 1))
        counted = [jnp.where((kc < here) | tie, 1.0, 0.0)]
        if at > 0:
            counted.insert(0, jnp.where(kc < key[:, :at], 1.0, 0.0))
        if end < ROWS:
            counted.append(jnp.where(kc <= key[:, end:], 1.0, 0.0))
        rank = rank + jnp.concatenate(
            [jnp.sum(x, axis=0, keepdims=True) for x in counted], axis=1
        )
    rank = rank.astype(jnp.int32)
    x = jnp.where(live, innov[...], 0.0)
    quarter = jnp.where(live, scale * 0.25, 0.0)
    m = jnp.concatenate([along, key, quarter, err], axis=0)
    xh, xr = x.astype(bf16), x - x.astype(bf16).astype(f32)
    xm, xl = split(xr)
    mh, mr = m.astype(bf16).astype(f32), m - m.astype(bf16).astype(f32)
    mm = mr.astype(bf16).astype(f32)
    ml = mr - mm
    metas = jnp.concatenate([mh, mm, ml, jnp.zeros((52, ROWS), f32)], axis=0).astype(bf16)
    data = jnp.concatenate([xh, xm, xl, metas], axis=0)
    pick = jnp.where(rank == iota((ROWS, 1), 0), 1.0, 0.0).astype(bf16)
    ordered = dot(pick, data, 1, 1)
    step = 256
    for b in range(ROWS // step):
        y = ordered[b * step : (b + 1) * step, :]
        t0, t1 = y[:, :128], y[:, 128:]
        r = t0 + pltpu.roll(t0, 64, 1) + t1
        c = t1 + pltpu.roll(t1, 124, 1) + pltpu.roll(t1, 120, 1)
        rows = pl.ds(b * step, step)
        col_out[rows, :] = c
        along_out[rows, :] = jnp.broadcast_to(c[:, 64:65], (step, 128))
        across_out[rows, :] = jnp.broadcast_to(c[:, 65:66], (step, 128))
        u = r * c[:, 66:67]
        for s in range(2):

            @pl.when(g % 2 == s)
            def _(s=s, r=r, u=u, rows=rows):
                res_out[0, rows, s * ENS : (s + 1) * ENS] = r[:, :ENS]
                wres_out[0, rows, s * ENS : (s + 1) * ENS] = u[:, :ENS]

        row_out[0:4, rows] = jnp.transpose(c)[64:68, :]
    row_out[4:5, :] = rank.astype(f32)
    lane = iota((1, ROWS), 1)
    bound = jnp.where(lane == PAIR_AT, pair[g, 0], jnp.where(lane == PAIR_AT + 1, pair[g, 1], 0))
    bound = bound.astype(f32)
    bound = jnp.where(lane == LIVE_AT, ((count[g] + BLK - 1) // BLK).astype(f32), bound)
    for b in range(NB):
        first = row_out[1:2, b * BLK : b * BLK + 1]
        last = row_out[1:2, (b + 1) * BLK - 1 : (b + 1) * BLK]
        bound = jnp.where(lane == b, first, bound)
        bound = jnp.where(lane == NB + b, jnp.minimum(last, TOP), bound)
    row_out[5:8, :] = jnp.broadcast_to(bound, (3, ROWS))
    for s in range(2):

        @pl.when(g % 2 == s)
        def _(s=s):
            for b in range(NB):
                wres_out[0, meta_rows(s * NB + b), :] = row_out[:, b * BLK : (b + 1) * BLK]


def meta_rows(block):
    return pl.ds(ROWS + 8 * block, 8)


def unpack_meta(dst, first, packed):
    for b in range(2 * NB):
        dst[:, pl.ds((first + b) * BLK, BLK)] = packed[0, meta_rows(b), :]


def load_split(dst, first, packed):
    lane = iota((1, 128), 1) < ENS
    hi = packed.astype(bf16).astype(f32)
    lo = packed - hi
    dst[pl.ds(first, ROWS), :] = jnp.where(lane, hi, pltpu.roll(lo, 64, 1)).astype(bf16)
    dst[pl.ds(first + ROWS, ROWS), :] = jnp.where(lane, pltpu.roll(hi, 64, 1), lo).astype(bf16)


def list_pairs(todo, n, rows, row_at, cols, col_at, offset, go):
    jlo = [cols[7, j] for j in range(NB)]
    jhi = [cols[7, NB + j] for j in range(NB)]

    def row_step(i, n):
        lo = rows[7, i] - MARGIN
        hi = rows[7, NB + i] + MARGIN
        base = row_at + i + 4096 * (offset + REACH)
        for j in range(NB):
            todo[n] = base + 64 * (col_at + j)
            n = n + jnp.where((jlo[j] <= hi) & (jhi[j] >= lo), 1, 0)
        return n

    live = rows[7, LIVE_AT].astype(jnp.int32)
    if go is not None:
        live = jnp.where(go > 0.5, live, 0)
    return lax.fori_loop(0, live, row_step, n)


def run_pairs(todo, start, n, alongs, acrosses, row_meta, halves, acc):
    trash = 32
    for u in range(UNROLL):
        todo[n + u] = trash + 4096 * REACH

    def group(t, _):
        out = []
        for u in range(UNROLL):
            code = todo[start + t * UNROLL + u]
            i = code & 63
            j = (code >> 6) & 63
            shift = ((code >> 12) - REACH).astype(f32)
            im = jnp.minimum(i, trash - 1)
            ri = pl.ds(pl.multiple_of(im * BLK, BLK), BLK)
            cj = pl.ds(pl.multiple_of(j * BLK, BLK), BLK)
            da = (row_meta[0:1, cj] + shift) - alongs[ri, :]
            db = row_meta[1:2, cj] - acrosses[ri, :]
            s = jnp.minimum(jnp.maximum(da * da + db * db, 1e-30), 1.0)
            q = s * lax.rsqrt(s)
            t1 = 1.0 - q
            t2 = t1 * t1
            phi = t2 * t2 * (4.0 * q + 1.0)
            hi, lo = split(phi)
            w = halves[cj, :]
            out.append(
                (i, dot(jnp.concatenate([hi, lo], axis=1), jnp.concatenate([w, w], axis=0)))
            )
        for i, val in out:
            ro = pl.ds(pl.multiple_of(i * BLK, BLK), BLK)
            acc[ro, :] += val
        return 0

    lax.fori_loop(0, (n - start + UNROLL - 1) // UNROLL, group, 0)


def fold(acc, first):
    a = acc[pl.ds(first, ROWS), :]
    b = acc[pl.ds(first + ROWS, ROWS), :]
    lane = iota((1, 128), 1) < ENS
    return jnp.where(lane, a + pltpu.roll(a, 64, 1), b + pltpu.roll(b, 64, 1))


def flag(bounds, d):
    return bounds[7, PAIR_AT + d - 1]


def fetch_bounds(row_meta, halos, scalars, sem):
    sources = [row_meta.at[:, pl.ds(g * ROWS, BLK)] for g in range(row_meta.shape[1] // ROWS)]
    for ref in halos:
        sources += [ref.at[0, meta_rows(g * NB), :] for g in range(REACH)]
    copies = [
        pltpu.make_async_copy(src, scalars.at[k], sem.at[k]) for k, src in enumerate(sources)
    ]
    for c in copies:
        c.start()
    for c in copies:
        c.wait()
    return [scalars.at[k] for k in range(len(copies))]


def near_kernel(regions, alongs, acrosses, row_meta, wres, out, scalars, sem, todo, halves, acc):
    bounds = fetch_bounds(row_meta, [], scalars, sem)
    for p in range(regions // 2):
        load_split(halves, 2 * p * ROWS, wres[p, pl.ds(0, ROWS), :])
    acc[...] = jnp.zeros_like(acc)
    n = jnp.int32(0)
    for g in range(regions):
        for d in range(-REACH, REACH + 1):
            h = g + d
            if 0 <= h < regions:
                go = None if d == 0 else flag(bounds[min(g, h)], abs(d))
                n = list_pairs(todo, n, bounds[g], g * NB, bounds[h], h * NB, d, go)
    run_pairs(todo, 0, n, alongs, acrosses, row_meta, halves, acc)
    out[...] = acc[: regions * ROWS, :]


def far_kernel(regions, col_meta, alongs, acrosses, row_meta, pres, nres, res, part, img_out, wimg_out,
               scalars, sem, todo, halves, acc, rowm):
    bounds = fetch_bounds(row_meta, [pres, nres], scalars, sem)
    pbounds, nbounds = bounds[regions : regions + REACH], bounds[regions + REACH :]
    span = REACH * ROWS
    load_split(halves, 0, pres[0, pl.ds(0, ROWS), :])
    load_split(halves, span, nres[0, pl.ds(0, ROWS), :])
    unpack_meta(rowm, 0, pres)
    unpack_meta(rowm, REACH * NB, nres)
    acc[: regions * ROWS, :] = part[...]
    acc[regions * ROWS :, :] = jnp.zeros((BLK, 128), f32)
    n = jnp.int32(0)
    for g in range(REACH):
        for d in range(g + 1, REACH + 1):
            h = REACH + g - d
            n = list_pairs(todo, n, bounds[g], g * NB, pbounds[h], h * NB, -d, flag(pbounds[h], d))
    for k in range(REACH):
        g = regions - REACH + k
        for d in range(REACH - k, REACH + 1):
            h = g + d - regions
            n = list_pairs(todo, n, bounds[g], g * NB, nbounds[h], (REACH + h) * NB, d, flag(bounds[g], d))
    run_pairs(todo, 0, n, alongs, acrosses, rowm, halves, acc)
    lane = iota((1, 128), 1) < ENS
    for p in range(regions // 2):
        a = col_meta[pl.ds(2 * p * ROWS, ROWS), :]
        b = col_meta[pl.ds((2 * p + 1) * ROWS, ROWS), :]
        w = jnp.where(lane, a[:, 66:67], b[:, 66:67])
        e = jnp.where(lane, a[:, 67:68], b[:, 67:68])
        image = fold(acc, 2 * p * ROWS) * w + e * res[p]
        img_out[p] = image
        wimg_out[p] = image * w


def near2_kernel(regions, alongs, acrosses, row_meta, wimg, res, img, out, gram_out,
                 scalars, sem, todo, halves, acc):
    bounds = fetch_bounds(row_meta, [], scalars, sem)
    for p in range(regions // 2):
        load_split(halves, 2 * p * ROWS, wimg[p])
    acc[...] = jnp.zeros_like(acc)
    n = jnp.int32(0)
    for g in range(regions):
        n = list_pairs(todo, n, bounds[g], g * NB, bounds[g], g * NB, 0, None)
    run_pairs(todo, 0, n, alongs, acrosses, row_meta, halves, acc)
    acc[...] = acc[...] * 0.5
    n = jnp.int32(0)
    for g in range(regions):
        for d in range(1, REACH + 1):
            if g + d < regions:
                go = flag(bounds[g], d)
                n = list_pairs(todo, n, bounds[g], g * NB, bounds[g + d], (g + d) * NB, d, go)
    run_pairs(todo, 0, n, alongs, acrosses, row_meta, halves, acc)
    out[...] = acc[: regions * ROWS, :]
    lane = iota((1, 128), 1) < ENS
    gram = jnp.zeros((128, 128), f32)
    mixed = jnp.zeros((128, 128), f32)
    for p in range(regions // 2):
        r, i = res[p], img[p]
        one = jnp.where(lane, r, pltpu.roll(i, 64, 1))
        two = jnp.where(lane, pltpu.roll(r, 64, 1), i)
        for x in (one, two):
            hi, lo = split(x)
            gram = gram + dot(hi, hi, 0, 0)
            mixed = mixed + dot(hi, lo, 0, 0)
    gram = gram + mixed + jnp.transpose(mixed)
    gram_out[...] = gram


def far2_kernel(regions, col_meta, alongs, acrosses, row_meta, nres, nimg, img, part, gram, out,
                scalars, sem, todo, halves, acc, rowm):
    bounds = fetch_bounds(row_meta, [nres], scalars, sem)
    nbounds = bounds[regions:]
    load_split(halves, 0, nimg[0])
    unpack_meta(rowm, 0, nres)
    acc[: regions * ROWS, :] = part[...]
    acc[regions * ROWS :, :] = jnp.zeros((BLK, 128), f32)
    n = jnp.int32(0)
    for k in range(REACH):
        g = regions - REACH + k
        for d in range(REACH - k, REACH + 1):
            h = g + d - regions
            n = list_pairs(todo, n, bounds[g], g * NB, nbounds[h], h * NB, d, flag(bounds[g], d))
    run_pairs(todo, 0, n, alongs, acrosses, rowm, halves, acc)
    lane = iota((1, 128), 1) < ENS
    half = jnp.zeros((128, 128), f32)
    for p in range(regions // 2):
        a = col_meta[pl.ds(2 * p * ROWS, ROWS), :]
        b = col_meta[pl.ds((2 * p + 1) * ROWS, ROWS), :]
        w = jnp.where(lane, a[:, 66:67], b[:, 66:67])
        e = jnp.where(lane, a[:, 67:68], b[:, 67:68])
        ih, il = split(img[p])
        jh, jl = split(w * fold(acc, 2 * p * ROWS) + (0.5 * e) * img[p])
        half = half + dot(ih, jh, 0, 0) + dot(ih, jl, 0, 0) + dot(il, jh, 0, 0)
    out[:, 0:64] = gram[0:64, 0:64]
    out[:, 64:128] = gram[0:64, 64:128]
    out[:, 128:192] = gram[64:128, 64:128]
    out[:, 192:256] = half[0:64, 0:64] + half[64:128, 64:128]


def slot_kernel(count, row_meta, innov, img, both_out):
    g = pl.program_id(0)
    live = iota((1, ROWS), 1) < count[g]
    r = jnp.where(live, innov[...], 0.0)
    t = jnp.transpose(img[0])
    t = jnp.where(g % 2 == 0, t[:ENS, :], t[ENS:, :])
    hi, lo = split(t)
    lhs = jnp.concatenate([hi, lo], axis=0)
    rank = row_meta[4:5, :].astype(jnp.int32)
    put = jnp.where(rank == iota((ROWS, 1), 0), 1.0, 0.0).astype(bf16)
    total = dot(lhs, put)
    both_out[...] = jnp.concatenate([r, total[:ENS, :] + total[ENS:, :]], axis=0)


def column_kernel(raw, both, sums_out):
    hi, lo = split(both[...] * raw[4:5, :])
    lhs = jnp.concatenate([hi, lo], axis=0)
    owner = raw[5:6, :].astype(jnp.int32)

    @pl.when(pl.program_id(0) == 0)
    def _():
        sums_out[...] = jnp.zeros_like(sums_out)

    step = 512
    for b in range(2 * COLS_DEV // step):
        own = jnp.where(owner == iota((step, 1), 0) + b * step, 1.0, 0.0).astype(bf16)
        y = dot(lhs, own, 1, 1)
        sums_out[:, b * step : (b + 1) * step] += y[: 2 * ENS, :] + y[2 * ENS :, :]


def eliminate(pairs):
    work = [jnp.concatenate([a, b], axis=1) for a, b in pairs]
    index = iota((ENS, 2 * ENS), 0)
    for k in range(0, ENS, GROUP):
        for p in range(len(work)):
            a = work[p]
            cols = [jnp.broadcast_to(a[:, k + c : k + c + 1], a.shape) for c in range(GROUP)]
            rows = [a[k + i : k + i + 1, :] for i in range(GROUP)]
            e = [[cols[c][k + i : k + i + 1, :] for c in range(GROUP)] for i in range(GROUP)]
            inv = []
            for c in range(GROUP):
                inv.append(1.0 / e[c][c])
                for i in range(c + 1, GROUP):
                    ratio = e[i][c] * inv[c]
                    for j in range(c + 1, GROUP):
                        e[i][j] = e[i][j] - ratio * e[c][j]
                    rows[i] = rows[i] - ratio * rows[c]
            for c in reversed(range(GROUP)):
                for j in range(c + 1, GROUP):
                    rows[c] = rows[c] - e[c][j] * rows[j]
                rows[c] = rows[c] * inv[c]
            for c in range(GROUP):
                a = a - cols[c] * rows[c]
            for c in range(GROUP):
                a = jnp.where(index == k + c, rows[c], a)
            work[p] = a
    return [a[:, ENS:] for a in work]


def finish_kernel(gram, both, sums, carried, weights_out, incr_out):
    g = gram[...]
    hd = functools.partial(dot, precision=highest)

    def sym(a):
        return 0.5 * (a + jnp.transpose(a))

    n0 = sym(g[:, 0:64])
    k0 = sym(g[:, 64:128])
    m0 = sym(g[:, 128:192])
    l0 = g[:, 192:256] + jnp.transpose(g[:, 192:256])
    eye = jnp.where(iota((ENS, ENS), 0) == iota((ENS, ENS), 1), 1.0, 0.0)
    s0, inv = eliminate([(k0, n0), (n0, eye)])
    s0t = jnp.transpose(s0)
    ks = hd(k0, s0)
    ms = hd(m0, s0)
    n1 = sym(n0 - ks - jnp.transpose(ks) + hd(s0t, ms))
    b = eye + hd(inv, n1)
    bt = jnp.transpose(b)
    cross = hd(bt, ms)
    c1 = sym(hd(bt, hd(k0, b)) - cross - jnp.transpose(cross) + hd(s0t, hd(l0, s0)))
    (s1,) = eliminate([(c1, n1)])
    mix = jnp.concatenate([s0 + hd(b, s1), -hd(s0, s1)], axis=0)
    mt = jnp.transpose(mix)
    hi, lo = split(mt)
    lhs = jnp.concatenate([hi, hi, lo], axis=1)

    def apply(x):
        xh, xl = split(x)
        return dot(lhs, jnp.concatenate([xh, xl, xh], axis=0))

    step = 512
    for c in range(weights_out.shape[1] // step):
        at = pl.ds(c * step, step)
        weights_out[:, at] = apply(both[:, at])
    for c in range(COLS_DEV // step):
        at = pl.ds(c * step, step)
        incr_out[:, at] = apply(sums[:, at] + carried[:, at])


def on_device(innovation, obs_along, obs_across, obs_scale, obs_error, obs_gain, pair_live, obs_count, col_owner):
    regions = obs_count.shape[0]
    local = regions * ROWS
    packs = regions // 2
    span = REACH * ROWS
    total_cols = COLS_DEV * lax.axis_size(AXES)
    owner = (col_owner - lax.axis_index(AXES) * COLS_DEV) % total_cols
    zero = jnp.zeros((local,), f32)
    raw = jnp.stack(
        [obs_along, obs_across, obs_scale, obs_error, obs_gain, owner.astype(f32), zero, zero]
    )
    shape = jax.ShapeDtypeStruct
    packed = shape((packs, ROWS, 128), f32)
    row_spec = pl.BlockSpec((8, ROWS), lambda g: (0, g))
    pack_spec = pl.BlockSpec((1, ROWS, 128), lambda g: (g // 2, 0, 0))
    held = ROWS + 16 * NB
    held_spec = pl.BlockSpec((1, held, 128), lambda g: (g // 2, 0, 0))
    member_spec = pl.BlockSpec((ENS, ROWS), lambda g: (0, g))
    row_meta, col_meta, alongs, acrosses, res, wres = pl.pallas_call(
        sort_kernel,
        grid=(regions,),
        in_specs=[SMEM, SMEM, row_spec, member_spec],
        out_specs=[row_spec] + [pl.BlockSpec((ROWS, 128), lambda g: (g, 0))] * 3 + [pack_spec, held_spec],
        out_shape=[shape((8, local), f32)] + [shape((local, 128), f32)] * 3 + [packed, shape((packs, held, 128), f32)],
        compiler_params=params(24),
        name="order",
    )(obs_count, pair_live, raw, innovation)

    pres = from_behind(wres[packs - 1 :], 1)
    nres = from_behind(wres[:1], -1)
    def scratch(blocks):
        halos = regions + 2 * REACH
        return [
            pltpu.SMEM((halos, 8, BLK), f32),
            pltpu.SemaphoreType.DMA((halos,)),
            pltpu.SMEM((20 * 64 + 8,), jnp.int32),
            pltpu.VMEM((blocks * ROWS, 128), bf16),
            pltpu.VMEM((local + BLK, 128), f32),
        ]

    plain = shape((local, 128), f32)

    part = pl.pallas_call(
        functools.partial(near_kernel, regions),
        in_specs=[VMEM] * 4,
        out_specs=VMEM,
        out_shape=plain,
        scratch_shapes=scratch(regions),
        compiler_params=params(24),
        cost_estimate=cost(int(4e9), int(2e7)),
        name="near",
    )(alongs, acrosses, row_meta, wres)
    img, wimg = pl.pallas_call(
        functools.partial(far_kernel, regions),
        in_specs=[VMEM] * 8,
        out_specs=[VMEM, VMEM],
        out_shape=[packed, packed],
        scratch_shapes=scratch(2 * REACH) + [pltpu.VMEM((8, 2 * span), f32)],
        compiler_params=params(24),
        name="far",
    )(col_meta, alongs, acrosses, row_meta, pres, nres, res, part)
    nimg = from_behind(wimg[:1], -1)
    part2, gram = pl.pallas_call(
        functools.partial(near2_kernel, regions),
        in_specs=[VMEM] * 6,
        out_specs=[VMEM, VMEM],
        out_shape=[plain, shape((128, 128), f32)],
        scratch_shapes=scratch(regions),
        compiler_params=params(24),
        cost_estimate=cost(int(4e9), int(2e7)),
        name="near_again",
    )(alongs, acrosses, row_meta, wimg, res, img)
    gram = pl.pallas_call(
        functools.partial(far2_kernel, regions),
        in_specs=[VMEM] * 9,
        out_specs=VMEM,
        out_shape=shape((ENS, 4 * ENS), f32),
        scratch_shapes=scratch(REACH) + [pltpu.VMEM((8, span), f32)],
        compiler_params=params(24),
        name="far_again",
    )(col_meta, alongs, acrosses, row_meta, nres, nimg, img, part2, gram)

    both_spec = pl.BlockSpec((2 * ENS, ROWS), lambda g: (0, g))
    both = pl.pallas_call(
        slot_kernel,
        grid=(regions,),
        in_specs=[SMEM, row_spec, member_spec, pack_spec],
        out_specs=both_spec,
        out_shape=shape((2 * ENS, local), f32),
        compiler_params=params(24),
        cost_estimate=cost(int(4e9), int(1e7)),
        name="slots",
    )(obs_count, row_meta, innovation, img)

    def columns(values):
        return pl.pallas_call(
            column_kernel,
            grid=(regions,),
            in_specs=[row_spec, both_spec],
            out_specs=pl.BlockSpec((2 * ENS, 2 * COLS_DEV), lambda g: (0, 0)),
            out_shape=shape((2 * ENS, 2 * COLS_DEV), f32),
            compiler_params=params(24),
            cost_estimate=cost(int(4e9), int(1e7)),
            name="columns",
        )(raw, values)

    gram, both, sums = all_sum(gram, both, columns)
    carried = from_behind(sums[:, COLS_DEV:], 1)
    return tuple(
        pl.pallas_call(
            finish_kernel,
            in_specs=[VMEM] * 4,
            out_specs=[VMEM, VMEM],
            out_shape=[shape((ENS, local), f32), shape((ENS, COLS_DEV), f32)],
            compiler_params=params(24),
            name="finish",
        )(gram, both, sums, carried)
    )


def solution(mesh):
    row = P(None, AXES)
    vec = P(AXES)
    in_specs = (row, vec, vec, vec, vec, vec, P(AXES, None), vec, vec)
    return jax.shard_map(
        on_device, mesh=mesh, in_specs=in_specs, out_specs=(row, row), check_vma=False
    )
```
